32 devices in a mesh: blk: 2 (over core), leaf: 16 (over z, y, x).
Axes of the slice: x: 2, y: 2, z: 4, core: 2. Of those that a mesh axis runs over, the one named last changes fastest.
Arguments:
- positions: float32 [3, 16, 2, 512], P(None, 'leaf', 'blk'), may hold values from 0 to 32, as said below
- panel_areas: float32 [16, 2, 512], P('leaf', 'blk'), may hold values from 0.5 to 2
- probe_cols: bfloat16 [576, 16, 2, 512], P(None, 'leaf', 'blk'), may hold values from -5 to 5
- full_sketch: bfloat16 [576, 16, 2, 512], P(None, 'leaf', 'blk'), may hold values from -3 to 3
- tree_order: int32 [16, 2, 512], P('leaf', 'blk'), may hold values from 0 to 511, each once within a row
- leaf_basis: bfloat16 [16, 2, 512, 512], P('leaf', 'blk'), may hold values from -0.1875 to 0.1875
- transfer_mats: bfloat16 [16, 3, 512, 512], P('leaf'), may hold values from -0.1875 to 0.1875
Outputs:
- offdiag_sketch: bfloat16 [576, 16, 2, 512], P(None, 'leaf', 'blk')
- nested_sketch: float32 [16, 2, 576, 512], P('leaf')
The draws below stay inside these ranges and needn't reach their ends.
Inputs may be any that keep to these rules, and one draw needn't show every extreme that they name: `positions`: each leaf's panel centres lie on a surface patch of 32 by 32 mean panel widths. `tree_order`: along the last dimension, each row names every one of the 512 panels of its block once.
All inputs are finite; a program needn't handle non-finite values.
Results may differ from the reference program's by a relative error of at most 0.0046.
Values sent between devices are 32-bit elements; how exact they have to be, the bound alone decides.
A program may use at most 64 MiB of HBM per device.

```python
import math
import jax
import jax.numpy as jnp
from jax import lax

GRID = 32
R = 576
Q = 512
LEVELS = 3
P_DEV = 512
NODES = 16
BLOCKS = 2
N_BLK = 2


def draw_positions(key, part):
    cell_count = BLOCKS * P_DEV
    key_list = jax.random.split(key, 4)
    leaf_keys = jax.random.split(key_list[0], NODES)
    counting = jnp.broadcast_to(jnp.arange(cell_count, dtype=jnp.int32), (NODES, cell_count))
    cell_order = jax.vmap(jax.random.permutation)(leaf_keys, counting)
    column = cell_order % GRID
    row_index = cell_order // GRID
    jitter = jax.random.uniform(key_list[1], (2, NODES, cell_count), jnp.float32, -0.5, 0.5)
    roughness = jax.random.uniform(key_list[2], (NODES, cell_count), jnp.float32, 0.0, 0.5)
    height = jax.random.randint(key_list[3], (NODES, cell_count), 0, 2).astype(jnp.float32) + roughness
    first_coord = column.astype(jnp.float32) + 0.5 + jitter[0]
    second_coord = row_index.astype(jnp.float32) + 0.5 + jitter[1]
    stacked = jnp.stack([first_coord, second_coord, height], axis=0)
    return stacked.reshape(3, NODES, BLOCKS, P_DEV)


def level_of(key, shape, shards, least, largest):
    loudness, own = 1.0, jax.random.fold_in(key, 6)
    for position, blocks in shards:
        draws = jnp.exp(jax.random.uniform(jax.random.fold_in(own, position), (blocks,), jnp.float32, least / len(shards), largest / len(shards)))
        loudness = loudness * jnp.repeat(draws, shape[position] // blocks).reshape([-1 if axis == position else 1 for axis in range(len(shape))])
    return loudness


def scatter_about(own_key, extent, scale, most, pieces=(), kind=jnp.bfloat16):
    array = jax.random.normal(own_key, extent, jnp.float32) * scale
    if len(pieces) > 0:
        array = level_of(own_key, extent, pieces, -0.22, 0.18) * array
    return jnp.clip(array, min=-most, max=most).astype(kind)


def setup_inputs(seed: int = 0) -> dict:
    splits = jax.random.split(jax.random.key(seed), 8)
    positions = draw_positions(jax.random.fold_in(splits[7], 71), 0)
    panel_areas = jnp.clip(jnp.exp(math.log(2.0) - 1.3862944 * jax.random.uniform(splits[1], (NODES, BLOCKS, P_DEV), jnp.float32) ** level_of(splits[1], (NODES, BLOCKS, P_DEV), ((0, 16), (1, 2)), -0.2, 0.2)), 0.5, 2.0)
    probe_cols = scatter_about(splits[2], (R, NODES, BLOCKS, P_DEV), 1.0, 5.0, ((1, 16), (2, 2)))
    full_sketch = scatter_about(splits[3], (R, NODES, BLOCKS, P_DEV), 0.5, 3.0, ((1, 16), (2, 2)))
    tree_order = jax.vmap(lambda own: jax.random.permutation(own, P_DEV))(jax.random.split(splits[4], NODES * BLOCKS)).reshape((NODES, BLOCKS, P_DEV)).astype(jnp.int32)
    leaf_basis = scatter_about(splits[5], (NODES, BLOCKS, P_DEV, Q), (N_BLK * P_DEV) ** -0.5, 0.1875, ((0, 16), (1, 2)))
    transfer_mats = scatter_about(splits[6], (NODES, LEVELS, Q, Q), (2 * Q) ** -0.5, 0.1875, ((0, 16),))
    return {"positions": positions, "panel_areas": panel_areas, "probe_cols": probe_cols, "full_sketch": full_sketch, "tree_order": tree_order, "leaf_basis": leaf_basis, "transfer_mats": transfer_mats}


inv_four_pi = 1.0 / (4.0 * math.pi)

def kernel_tile(target_pos, target_area, source_pos, source_area):
    distance = jnp.zeros((target_pos.shape[1], source_pos.shape[1]), jnp.float32)
    for component in range(3):
        gap = target_pos[component][:, None] - source_pos[component][None, :]
        distance = distance + gap * gap
    soft = distance + 0.5 * (target_area[:, None] + source_area[None, :])
    return (inv_four_pi * lax.rsqrt(soft)).astype(jnp.bfloat16)

def reference(positions, panel_areas, probe_cols, full_sketch, tree_order, leaf_basis, transfer_mats):
    node_count = positions.shape[1]
    block_total = positions.shape[2]
    panels = positions.shape[3]
    probe_count = probe_cols.shape[0]
    block_size = min(512, panels)
    scaled = (panel_areas[None].astype(jnp.float32) * probe_cols.astype(jnp.float32)).astype(jnp.bfloat16)

    def leaf_near(items):
        leaf_pos, leaf_area, leaf_scaled = items
        source_pos = leaf_pos.reshape(3, -1)
        source_area = leaf_area.reshape(-1)
        source_scaled = leaf_scaled.reshape(probe_count, -1)
        block_count = source_pos.shape[1] // block_size
        target_blocks = jnp.transpose(source_pos.reshape(3, block_count, block_size), (1, 0, 2))
        area_blocks = source_area.reshape(block_count, block_size)

        def one_block(entry):
            block_pos, block_area = entry
            kernel = kernel_tile(block_pos, block_area, source_pos, source_area)
            return lax.dot_general(source_scaled, kernel, (((1,), (1,)), ((), ())), preferred_element_type=jnp.float32)
        sums = lax.map(one_block, (target_blocks, area_blocks))
        return jnp.transpose(sums, (1, 0, 2)).reshape(probe_count, block_total, panels)
    near_sum = lax.map(leaf_near, (jnp.moveaxis(positions, 1, 0), panel_areas, jnp.moveaxis(scaled, 1, 0)))
    near_sum = jnp.moveaxis(near_sum, 0, 1)
    offdiag_sketch = (full_sketch.astype(jnp.float32) - near_sum).astype(jnp.bfloat16)
    sort_index = jnp.broadcast_to(tree_order[None].astype(jnp.int32), offdiag_sketch.shape)
    sorted_off = jnp.take_along_axis(offdiag_sketch, sort_index, axis=3)
    sorted_probe = jnp.take_along_axis(probe_cols, sort_index, axis=3)

    def compress(items):
        off_leaf, probe_leaf, basis_leaf = items
        basis_flat = basis_leaf.reshape(-1, basis_leaf.shape[2])
        first = jnp.dot(off_leaf.reshape(probe_count, -1), basis_flat, preferred_element_type=jnp.float32)
        second = jnp.dot(probe_leaf.reshape(probe_count, -1), basis_flat, preferred_element_type=jnp.float32)
        return (first, second)
    sketch, probes = lax.map(compress, (jnp.moveaxis(sorted_off, 1, 0), jnp.moveaxis(sorted_probe, 1, 0), leaf_basis))
    for tree_level in range(transfer_mats.shape[1]):
        level_mats = transfer_mats[:, tree_level].astype(jnp.float32)
        partner = jnp.arange(node_count, dtype=jnp.int32) ^ 1 << tree_level
        sketch_proj = jnp.einsum('nrq,nqk->nrk', sketch, level_mats, precision=lax.Precision.HIGHEST)
        probe_proj = jnp.einsum('nrq,nqk->nrk', probes, level_mats, precision=lax.Precision.HIGHEST)
        sketch = sketch_proj + sketch_proj[partner]
        probes = probe_proj + probe_proj[partner]
    return (offdiag_sketch, jnp.stack([sketch, probes], axis=1))
```

```python
import functools
import math

import jax
import jax.numpy as jnp
from jax import lax
from jax.experimental import pallas as pl
from jax.experimental.pallas import tpu as pltpu
from jax.sharding import PartitionSpec as P

MESH = pl.DeviceIdType.MESH
inv_four_pi = 1.0 / (4.0 * math.pi)


def chunk_rows(share):
    return max(rows for rows in range(8, min(share, 72) + 1, 8) if share % rows == 0)


def leaf_partner(me, level):
    step = 2**level
    return me + step * (1 - 2 * lax.rem(lax.div(me, step), 2))


def kernel(
    blocks, levels, chunk,
    pos_ref, area_ref, order_ref, probe_hbm, full_hbm, basis_hbm, mats_hbm,
    off_hbm, nested_hbm,
    probe, full, basis, mats, sorted_basis, tile, geo, geo_in, columns, scaled, scaled_in,
    near, off, part, part_in, going, coming, done,
    load_sem, off_sem, geo_send, geo_recv, scaled_send, scaled_recv, part_send, part_recv,
    level_send, level_recv, done_send, done_recv, done_local,
):
    count, panels = probe.shape
    share = count // blocks
    per_half = share // chunk
    total = 2 * per_half
    my_blk = lax.axis_index("blk")
    my_leaf = lax.axis_index("leaf")
    peers = [lax.rem(my_blk + distance, blocks) for distance in range(1, blocks)]
    partners = [leaf_partner(my_leaf, level) for level in range(levels)]

    loads = [
        pltpu.make_async_copy(source, target, load_sem.at[index])
        for index, (source, target) in enumerate(
            [(probe_hbm, probe), (basis_hbm, basis), (mats_hbm, mats), (full_hbm, full)]
        )
    ]
    for load in loads:
        load.start()

    barrier = pltpu.get_barrier_semaphore()
    for peer in peers:
        pl.semaphore_signal(barrier, inc=1, device_id={"blk": peer}, device_id_type=MESH)
    for partner in partners:
        pl.semaphore_signal(barrier, inc=1, device_id={"leaf": partner}, device_id_type=MESH)

    def to_peers(source, target, send, recv):
        return [
            pltpu.make_async_remote_copy(
                src_ref=source, dst_ref=target.at[index], send_sem=send.at[index],
                recv_sem=recv.at[index], device_id={"blk": peer}, device_id_type=MESH,
            )
            for index, peer in enumerate(peers)
        ]

    def rows_of_peer(half):
        return [
            pltpu.make_async_remote_copy(
                src_ref=part.at[half, pl.ds(pl.multiple_of(peer * share, 8), share)],
                dst_ref=part_in.at[half, index],
                send_sem=part_send.at[half, index], recv_sem=part_recv.at[half, index],
                device_id={"blk": peer}, device_id_type=MESH,
            )
            for index, peer in enumerate(peers)
        ]

    geo_copies = to_peers(geo, geo_in, geo_send, geo_recv)
    scaled_copies = to_peers(scaled, scaled_in, scaled_send, scaled_recv)
    part_copies = [rows_of_peer(0), rows_of_peer(1)]

    def chunk_slice(position):
        return pl.ds(pl.multiple_of(position * chunk, 8), chunk)

    def exchange(level, position):
        rows = chunk_slice(position)
        return pltpu.make_async_remote_copy(
            src_ref=going.at[level, rows], dst_ref=coming.at[level, rows],
            send_sem=level_send.at[level, position], recv_sem=level_recv.at[level, position],
            device_id={"leaf": partners[level]}, device_id_type=MESH,
        )

    def result_rows(position):
        half = 1 - lax.div(position, per_half)
        start = my_blk * share + lax.rem(position, per_half) * chunk
        return nested_hbm.at[0, half, pl.ds(pl.multiple_of(start, 8), chunk)]

    def result_copies(position):
        return [
            pltpu.make_async_remote_copy(
                src_ref=done.at[chunk_slice(position)], dst_ref=result_rows(position),
                send_sem=done_send.at[index, position], recv_sem=done_recv.at[index, position],
                device_id={"blk": peer}, device_id_type=MESH,
            )
            for index, peer in enumerate(peers)
        ]

    def local_result(position):
        return pltpu.make_async_copy(
            done.at[chunk_slice(position)], result_rows(position), done_local.at[position]
        )

    def project(value, level):
        high = value.astype(jnp.bfloat16).astype(jnp.float32)
        both = jnp.concatenate([high, value - high], axis=0).astype(jnp.bfloat16)
        product = jnp.dot(both, mats[level], preferred_element_type=jnp.float32)
        return product[:chunk] + product[chunk:]

    def first_level(half, inner):
        start = pl.multiple_of(my_blk * share + inner * chunk, 8)
        value = part[half, pl.ds(start, chunk), :]
        for index in range(blocks - 1):
            value = value + part_in[half, index, chunk_slice(inner), :]
        position = half * per_half + inner
        going[0, chunk_slice(position), :] = project(value, 0)
        exchange(0, position).start()

    def joined(level, position):
        exchange(level, position).wait_recv()
        rows = chunk_slice(position)
        return going[level, rows, :] + coming[level, rows, :]

    def next_level(level, position):
        going[level, chunk_slice(position), :] = project(joined(level - 1, position), level)
        exchange(level, position).start()

    def finish(position):
        done[chunk_slice(position), :] = joined(levels - 1, position)
        for copy in result_copies(position):
            copy.start()
        local_result(position).start()

    def kernel_tile(source):
        step = min(128, panels)

        def some_rows(index, carry):
            rows = pl.ds(pl.multiple_of(index * step, step), step)
            values = columns[rows, :]
            distance = jnp.zeros((step, panels), jnp.float32)
            for component in range(3):
                gap = geo[component : component + 1, :] - values[:, component : component + 1]
                distance = distance + gap * gap
            soft = distance + 0.5 * (geo[3:4, :] + values[:, 3:4])
            tile[rows, :] = (inv_four_pi * lax.rsqrt(soft)).astype(jnp.bfloat16)
            return carry

        columns[...] = jnp.transpose(source)
        lax.fori_loop(0, panels // step, some_rows, 0)

    geo[...] = jnp.zeros_like(geo)
    geo[0:3, :] = pos_ref[...]
    geo[3:4, :] = area_ref[...]
    places = lax.broadcasted_iota(jnp.int32, (panels, panels), 0)
    chosen = jnp.where(places == order_ref[...], 1.0, 0.0).astype(jnp.bfloat16)
    loads[1].wait()
    sorted_basis[...] = jnp.dot(
        chosen, basis[...], preferred_element_type=jnp.float32
    ).astype(jnp.bfloat16)
    loads[0].wait()
    part[0] = jnp.dot(probe[...], sorted_basis[...], preferred_element_type=jnp.float32)
    pl.semaphore_wait(barrier, blocks - 1 + levels)
    for copy in part_copies[0] + geo_copies:
        copy.start()
    scaled[...] = (
        (area_ref[...] * probe[...].astype(jnp.float32)).astype(jnp.bfloat16).astype(jnp.float32)
    )
    for copy in scaled_copies:
        copy.start()
    kernel_tile(geo[...])
    loads[2].wait()
    for copy in part_copies[0]:
        copy.wait_recv()

    def first_probe(inner, carry):
        first_level(0, inner)
        return carry

    lax.fori_loop(0, per_half, first_probe, 0)
    near[...] = jnp.dot(
        scaled[...].astype(jnp.bfloat16), tile[...], preferred_element_type=jnp.float32
    )
    for index in range(blocks - 1):
        geo_copies[index].wait_recv()
        kernel_tile(geo_in[index])
        scaled_copies[index].wait_recv()
        near[...] += jnp.dot(
            scaled_in[index].astype(jnp.bfloat16), tile[...], preferred_element_type=jnp.float32
        )
    loads[3].wait()
    off[...] = (full[...].astype(jnp.float32) - near[...]).astype(jnp.bfloat16)
    off_copy = pltpu.make_async_copy(off, off_hbm, off_sem.at[0])
    off_copy.start()
    if per_half > 2:
        next_level(1, 0)
    part[1] = jnp.dot(off[...], sorted_basis[...], preferred_element_type=jnp.float32)
    for copy in part_copies[1]:
        copy.start()
    for position in range(1, per_half - 2):
        next_level(1, position)
    for position in range(per_half - 3):
        next_level(2, position)
    for position in range(per_half - 4):
        finish(position)
    for copy in part_copies[1]:
        copy.wait_recv()

    def one_step(step, carry):
        @pl.when(step < total)
        def _():
            first_level(1, step - per_half)

        for level in range(1, levels):
            @pl.when((step >= level + 1) & (step < total + level + 1))
            def _(level=level):
                next_level(level, step - level - 1)

        @pl.when((step >= levels + 1) & (step < total + levels + 1))
        def _():
            finish(step - levels - 1)

        return carry

    lax.fori_loop(per_half, total + levels + 1, one_step, 0)

    def settle(position, carry):
        for level in range(levels):
            exchange(level, position).wait_send()
        for copy in result_copies(position):
            copy.wait()
        local_result(position).wait()
        return carry

    lax.fori_loop(0, total, settle, 0)
    off_copy.wait()
    for copy in geo_copies + scaled_copies + part_copies[0] + part_copies[1]:
        copy.wait_send()


def shards(positions, panel_areas, probe_cols, full_sketch, tree_order, leaf_basis, transfer_mats):
    panels = positions.shape[3]
    count = probe_cols.shape[0]
    width = leaf_basis.shape[3]
    levels = transfer_mats.shape[1]
    blocks = lax.axis_size("blk")
    share = count // blocks
    chunk = chunk_rows(share)
    total = 2 * share // chunk
    f32, b16 = jnp.float32, jnp.bfloat16
    dma = pltpu.SemaphoreType.DMA
    whole = pl.BlockSpec(memory_space=pltpu.VMEM)
    anywhere = pl.BlockSpec(memory_space=pl.ANY)
    offdiag, nested = pl.pallas_call(
        functools.partial(kernel, blocks, levels, chunk),
        out_shape=(
            jax.ShapeDtypeStruct((count, panels), b16),
            jax.ShapeDtypeStruct((1, 2, count, width), f32),
        ),
        in_specs=[whole] * 3 + [anywhere] * 4,
        out_specs=(anywhere, anywhere),
        scratch_shapes=[
            pltpu.VMEM((count, panels), b16),
            pltpu.VMEM((count, panels), b16),
            pltpu.VMEM((panels, width), b16),
            pltpu.VMEM((levels, width, width), b16),
            pltpu.VMEM((panels, width), b16),
            pltpu.VMEM((panels, panels), b16),
            pltpu.VMEM((8, panels), f32),
            pltpu.VMEM((blocks - 1, 8, panels), f32),
            pltpu.VMEM((panels, 8), f32),
            pltpu.VMEM((count, panels), f32),
            pltpu.VMEM((blocks - 1, count, panels), f32),
            pltpu.VMEM((count, panels), f32),
            pltpu.VMEM((count, panels), b16),
            pltpu.VMEM((2, count, width), f32),
            pltpu.VMEM((2, blocks - 1, share, width), f32),
            pltpu.VMEM((levels, 2 * share, width), f32),
            pltpu.VMEM((levels, 2 * share, width), f32),
            pltpu.VMEM((2 * share, width), f32),
            dma((4,)), dma((1,)),
            dma((blocks - 1,)), dma((blocks - 1,)),
            dma((blocks - 1,)), dma((blocks - 1,)),
            dma((2, blocks - 1)), dma((2, blocks - 1)),
            dma((levels, total)), dma((levels, total)),
            dma((blocks - 1, total)), dma((blocks - 1, total)),
            dma((total,)),
        ],
        compiler_params=pltpu.CompilerParams(
            collective_id=0, has_side_effects=True, vmem_limit_bytes=48 * 2**20
        ),
    )(
        positions.reshape(3, panels),
        panel_areas.reshape(1, panels),
        tree_order.reshape(1, panels),
        probe_cols.reshape(count, panels),
        full_sketch.reshape(count, panels),
        leaf_basis.reshape(panels, width),
        transfer_mats.reshape(levels, width, width),
    )
    return (offdiag.reshape(count, 1, 1, panels), nested)


def solution(mesh):
    in_specs = (
        P(None, "leaf", "blk", None),
        P("leaf", "blk", None),
        P(None, "leaf", "blk", None),
        P(None, "leaf", "blk", None),
        P("leaf", "blk", None),
        P("leaf", "blk", None, None),
        P("leaf", None, None, None),
    )
    out_specs = (P(None, "leaf", "blk", None), P("leaf", None, None, None))
    return jax.shard_map(shards, mesh=mesh, in_specs=in_specs, out_specs=out_specs, check_vma=False)
```

```python
import functools
import math

import jax
import jax.numpy as jnp
from jax import lax
from jax.experimental import pallas as pl
from jax.experimental.pallas import tpu as pltpu
from jax.sharding import PartitionSpec as P

MESH = pl.DeviceIdType.MESH
inv_four_pi = 1.0 / (4.0 * math.pi)


def chunk_rows(share):
    return max(rows for rows in range(8, min(share, 48) + 1, 8) if share % rows == 0)


def leaf_partner(me, level):
    step = 2**level
    return me + step * (1 - 2 * lax.rem(lax.div(me, step), 2))


def kernel(
    blocks, levels, chunk,
    pos_hbm, area_hbm, order_hbm, probe_hbm, full_hbm, basis_hbm, mats_hbm,
    off, nested,
    order, probe, full, basis, mats, sorted_basis, tile, geo, geo_in, columns, scaled, scaled_in,
    near, part, part_in, going, coming,
    load_sem, geo_send, geo_recv, scaled_send, scaled_recv, part_send, part_recv,
    level_send, level_recv, done_send, done_recv,
):
    count, panels = probe.shape
    share = count // blocks
    per_half = share // chunk
    total = 2 * per_half
    my_blk = lax.axis_index("blk")
    my_leaf = lax.axis_index("leaf")
    peers = [lax.rem(my_blk + distance, blocks) for distance in range(1, blocks)]
    partners = [leaf_partner(my_leaf, level) for level in range(levels)]

    loads = [
        pltpu.make_async_copy(source, target, load_sem.at[index])
        for index, (source, target) in enumerate(
            [
                (order_hbm.at[0], order), (basis_hbm, basis), (probe_hbm, probe),
                (area_hbm.at[0], geo.at[pl.ds(3, 1)]),
            ]
            + [(pos_hbm.at[axis, 0], geo.at[pl.ds(axis, 1)]) for axis in range(3)]
            + [(mats_hbm, mats), (full_hbm, full)]
        )
    ]
    order_load, basis_load, probe_load, *geo_loads, mats_load, full_load = loads
    geo[...] = jnp.zeros_like(geo)
    for load in loads:
        load.start()

    barrier = pltpu.get_barrier_semaphore()
    for peer in peers:
        pl.semaphore_signal(barrier, inc=1, device_id={"blk": peer}, device_id_type=MESH)
    for partner in partners:
        pl.semaphore_signal(barrier, inc=1, device_id={"leaf": partner}, device_id_type=MESH)

    def to_peers(source, target, send, recv):
        return [
            pltpu.make_async_remote_copy(
                src_ref=source, dst_ref=target.at[index], send_sem=send.at[index],
                recv_sem=recv.at[index], device_id={"blk": peer}, device_id_type=MESH,
            )
            for index, peer in enumerate(peers)
        ]

    def part_copies(half, inner):
        start, size = (0, share) if inner is None else (inner * chunk, chunk)
        place = 0 if inner is None else inner
        return [
            pltpu.make_async_remote_copy(
                src_ref=part.at[half, pl.ds(pl.multiple_of(peer * share + start, 8), size)],
                dst_ref=part_in.at[half, index, pl.ds(pl.multiple_of(start, 8), size)],
                send_sem=part_send.at[half, index],
                recv_sem=part_recv.at[half, index, place],
                device_id={"blk": peer}, device_id_type=MESH,
            )
            for index, peer in enumerate(peers)
        ]

    geo_copies = to_peers(geo, geo_in, geo_send, geo_recv)
    scaled_copies = to_peers(scaled, scaled_in, scaled_send, scaled_recv)

    def chunk_slice(position):
        return pl.ds(pl.multiple_of(position * chunk, 8), chunk)

    def exchange(level, position):
        rows = chunk_slice(position)
        return pltpu.make_async_remote_copy(
            src_ref=going.at[level, rows], dst_ref=coming.at[level, rows],
            send_sem=level_send.at[level], recv_sem=level_recv.at[level, position],
            device_id={"leaf": partners[level]}, device_id_type=MESH,
        )

    def result_copies(half, rows):
        return [
            pltpu.make_async_remote_copy(
                src_ref=nested.at[0, 1 - half, rows], dst_ref=nested.at[0, 1 - half, rows],
                send_sem=done_send.at[half, index], recv_sem=done_recv.at[half, index],
                device_id={"blk": peer}, device_id_type=MESH,
            )
            for index, peer in enumerate(peers)
        ]

    def project(value, level):
        high = value.astype(jnp.bfloat16).astype(jnp.float32)
        both = jnp.concatenate([high, value - high], axis=0).astype(jnp.bfloat16)
        product = jnp.dot(both, mats[level], preferred_element_type=jnp.float32)
        return product[:chunk] + product[chunk:]

    def first_level(half, inner):
        for copy in part_copies(half, inner):
            copy.wait_recv()
        start = pl.multiple_of(my_blk * share + inner * chunk, 8)
        value = part[half, pl.ds(start, chunk), :]
        for index in range(blocks - 1):
            value = value + part_in[half, index, chunk_slice(inner), :]
        position = half * per_half + inner
        going[0, chunk_slice(position), :] = project(value, 0)
        exchange(0, position).start()

    def joined(level, position):
        exchange(level, position).wait_recv()
        rows = chunk_slice(position)
        return going[level, rows, :] + coming[level, rows, :]

    def next_level(level, position):
        going[level, chunk_slice(position), :] = project(joined(level - 1, position), level)
        exchange(level, position).start()

    def finish(position):
        half = lax.div(position, per_half)
        start = my_blk * share + lax.rem(position, per_half) * chunk
        rows = pl.ds(pl.multiple_of(start, 8), chunk)
        nested[0, 1 - half, rows, :] = joined(levels - 1, position)
        for copy in result_copies(half, rows):
            copy.start()

    def kernel_tile(source):
        step = min(128, panels)

        def some_rows(index, carry):
            rows = pl.ds(pl.multiple_of(index * step, step), step)
            values = columns[rows, :]
            distance = jnp.zeros((step, panels), jnp.float32)
            for component in range(3):
                gap = geo[component : component + 1, :] - values[:, component : component + 1]
                distance = distance + gap * gap
            soft = distance + 0.5 * (geo[3:4, :] + values[:, 3:4])
            tile[rows, :] = (inv_four_pi * lax.rsqrt(soft)).astype(jnp.bfloat16)
            return carry

        columns[...] = jnp.transpose(source)
        lax.fori_loop(0, panels // step, some_rows, 0)

    def send_part(half):
        def one(inner, carry):
            for copy in part_copies(half, inner):
                copy.start()
            return carry

        lax.fori_loop(0, per_half, one, 0)

    order_load.wait()
    places = lax.broadcasted_iota(jnp.int32, (panels, panels), 0)
    chosen = jnp.where(places == order[...], 1.0, 0.0).astype(jnp.bfloat16)
    basis_load.wait()
    sorted_basis[...] = jnp.dot(
        chosen, basis[...], preferred_element_type=jnp.float32
    ).astype(jnp.bfloat16)
    probe_load.wait()
    part[0] = jnp.dot(probe[...], sorted_basis[...], preferred_element_type=jnp.float32)
    pl.semaphore_wait(barrier, blocks - 1 + levels)
    send_part(0)
    for load in geo_loads:
        load.wait()
    scaled[...] = (
        (geo[3:4, :] * probe[...].astype(jnp.float32)).astype(jnp.bfloat16).astype(jnp.float32)
    )
    for copy in geo_copies + scaled_copies:
        copy.start()
    mats_load.wait()

    def first_probe(inner, carry):
        first_level(0, inner)
        return carry

    lax.fori_loop(0, per_half, first_probe, 0)
    kernel_tile(geo[...])
    near[...] = jnp.dot(
        scaled[...].astype(jnp.bfloat16), tile[...], preferred_element_type=jnp.float32
    )
    if per_half > 2:
        next_level(1, 0)
    for index in range(blocks - 1):
        geo_copies[index].wait_recv()
        kernel_tile(geo_in[index])
        scaled_copies[index].wait_recv()
        near[...] += jnp.dot(
            scaled_in[index].astype(jnp.bfloat16), tile[...], preferred_element_type=jnp.float32
        )
    full_load.wait()
    off[...] = (full[...].astype(jnp.float32) - near[...]).astype(jnp.bfloat16)
    part[1] = jnp.dot(off[...], sorted_basis[...], preferred_element_type=jnp.float32)
    send_part(1)
    for position in range(1, per_half - 2):
        next_level(1, position)
        for level in range(2, levels):
            if position >= 2 * level - 2:
                next_level(level, position - 2 * level + 2)

    def one_step(step, carry):
        @pl.when(step < total)
        def _():
            first_level(1, step - per_half)

        for level in range(1, levels):
            @pl.when((step >= 2 * level) & (step < total + 2 * level))
            def _(level=level):
                next_level(level, step - 2 * level)

        @pl.when((step >= 2 * levels) & (step < total + 2 * levels))
        def _():
            finish(step - 2 * levels)

        return carry

    lax.fori_loop(per_half, total + 2 * levels, one_step, 0)
    for level in range(levels):
        pltpu.make_async_remote_copy(
            src_ref=going.at[level], dst_ref=coming.at[level],
            send_sem=level_send.at[level], recv_sem=level_recv.at[level, 0],
            device_id={"leaf": partners[level]}, device_id_type=MESH,
        ).wait_send()
    for half in range(2):
        for copy in result_copies(half, pl.ds(0, share)):
            copy.wait()
        for copy in part_copies(half, None):
            copy.wait_send()
    for copy in geo_copies + scaled_copies:
        copy.wait_send()


def shards(positions, panel_areas, probe_cols, full_sketch, tree_order, leaf_basis, transfer_mats):
    panels = positions.shape[3]
    count = probe_cols.shape[0]
    width = leaf_basis.shape[3]
    levels = transfer_mats.shape[1]
    blocks = lax.axis_size("blk")
    share = count // blocks
    chunk = chunk_rows(share)
    total = 2 * share // chunk
    f32, b16 = jnp.float32, jnp.bfloat16
    dma = pltpu.SemaphoreType.DMA
    whole = pl.BlockSpec(memory_space=pltpu.VMEM)
    hbm = pl.BlockSpec(memory_space=pltpu.HBM)
    offdiag, nested = pl.pallas_call(
        functools.partial(kernel, blocks, levels, chunk),
        out_shape=(
            pltpu.VMEM((count, panels), b16),
            pltpu.VMEM((1, 2, count, width), f32),
        ),
        in_specs=[hbm] * 7,
        out_specs=(whole, whole),
        scratch_shapes=[
            pltpu.VMEM((1, panels), jnp.int32),
            pltpu.VMEM((count, panels), b16),
            pltpu.VMEM((count, panels), b16),
            pltpu.VMEM((panels, width), b16),
            pltpu.VMEM((levels, width, width), b16),
            pltpu.VMEM((panels, width), b16),
            pltpu.VMEM((panels, panels), b16),
            pltpu.VMEM((8, panels), f32),
            pltpu.VMEM((blocks - 1, 8, panels), f32),
            pltpu.VMEM((panels, 8), f32),
            pltpu.VMEM((count, panels), f32),
            pltpu.VMEM((blocks - 1, count, panels), f32),
            pltpu.VMEM((count, panels), f32),
            pltpu.VMEM((2, count, width), f32),
            pltpu.VMEM((2, blocks - 1, share, width), f32),
            pltpu.VMEM((levels, 2 * share, width), f32),
            pltpu.VMEM((levels, 2 * share, width), f32),
            dma((9,)),
            dma((blocks - 1,)), dma((blocks - 1,)),
            dma((blocks - 1,)), dma((blocks - 1,)),
            dma((2, blocks - 1)), dma((2, blocks - 1, total // 2)),
            dma((levels,)), dma((levels, total)),
            dma((2, blocks - 1)), dma((2, blocks - 1)),
        ],
        compiler_params=pltpu.CompilerParams(
            collective_id=0, has_side_effects=True, vmem_limit_bytes=58 * 2**20
        ),
    )(
        positions,
        panel_areas,
        tree_order,
        probe_cols.reshape(count, panels),
        full_sketch.reshape(count, panels),
        leaf_basis.reshape(panels, width),
        transfer_mats.reshape(levels, width, width),
    )
    return (offdiag.reshape(count, 1, 1, panels), nested)


def solution(mesh):
    in_specs = (
        P(None, "leaf", "blk", None),
        P("leaf", "blk", None),
        P(None, "leaf", "blk", None),
        P(None, "leaf", "blk", None),
        P("leaf", "blk", None),
        P("leaf", "blk", None, None),
        P("leaf", None, None, None),
    )
    out_specs = (P(None, "leaf", "blk", None), P("leaf", None, None, None))
    return jax.shard_map(shards, mesh=mesh, in_specs=in_specs, out_specs=out_specs, check_vma=False)
```

```python
import functools
import math

import jax
import jax.numpy as jnp
from jax import lax
from jax.experimental import pallas as pl
from jax.experimental.pallas import tpu as pltpu
from jax.sharding import PartitionSpec as P

MESH = pl.DeviceIdType.MESH
inv_four_pi = 1.0 / (4.0 * math.pi)


def chunk_rows(share):
    return max(rows for rows in range(8, min(share, 32) + 1, 8) if share % rows == 0)


def leaf_partner(me, level):
    step = 2**level
    return me + step * (1 - 2 * lax.rem(lax.div(me, step), 2))


def kernel(
    blocks, levels, chunk,
    pos_hbm, area_hbm, order_hbm, probe_hbm, full_hbm, basis_hbm, mats_hbm,
    off, nested,
    order, probe, full, basis, mats, sorted_basis, tile, geo, geo_in, columns, scaled, scaled_in,
    near, part, part_in, going, coming,
    load_sem, geo_send, geo_recv, scaled_send, scaled_recv, part_send, part_recv,
    level_send, level_recv, done_send, done_recv,
):
    count, panels = probe.shape
    share = count // blocks
    per_half = share // chunk
    total = 2 * per_half
    my_blk = lax.axis_index("blk")
    my_leaf = lax.axis_index("leaf")
    peers = [lax.rem(my_blk + distance, blocks) for distance in range(1, blocks)]
    partners = [leaf_partner(my_leaf, level) for level in range(levels)]

    loads = [
        pltpu.make_async_copy(source, target, load_sem.at[index])
        for index, (source, target) in enumerate(
            [
                (order_hbm.at[0], order), (basis_hbm, basis), (probe_hbm, probe),
                (area_hbm.at[0], geo.at[pl.ds(3, 1)]),
            ]
            + [(pos_hbm.at[axis, 0], geo.at[pl.ds(axis, 1)]) for axis in range(3)]
            + [(mats_hbm, mats), (full_hbm, full)]
        )
    ]
    order_load, basis_load, probe_load, *geo_loads, mats_load, full_load = loads
    barrier = pltpu.get_barrier_semaphore()
    for peer in peers:
        pl.semaphore_signal(barrier, inc=1, device_id={"blk": peer}, device_id_type=MESH)
    for partner in partners:
        pl.semaphore_signal(barrier, inc=1, device_id={"leaf": partner}, device_id_type=MESH)
    geo[...] = jnp.zeros_like(geo)
    for load in [order_load, basis_load, probe_load] + geo_loads:
        load.start()

    def to_peers(source, target, send, recv):
        return [
            pltpu.make_async_remote_copy(
                src_ref=source, dst_ref=target.at[index], send_sem=send.at[index],
                recv_sem=recv.at[index], device_id={"blk": peer}, device_id_type=MESH,
            )
            for index, peer in enumerate(peers)
        ]

    def part_copies(half, inner):
        start, size = (0, share) if inner is None else (inner * chunk, chunk)
        place = 0 if inner is None else inner
        return [
            pltpu.make_async_remote_copy(
                src_ref=part.at[half, pl.ds(pl.multiple_of(peer * share + start, 8), size)],
                dst_ref=part_in.at[half, index, pl.ds(pl.multiple_of(start, 8), size)],
                send_sem=part_send.at[half, index],
                recv_sem=part_recv.at[half, index, place],
                device_id={"blk": peer}, device_id_type=MESH,
            )
            for index, peer in enumerate(peers)
        ]

    geo_copies = to_peers(geo, geo_in, geo_send, geo_recv)
    scaled_copies = to_peers(scaled, scaled_in, scaled_send, scaled_recv)

    def chunk_slice(position):
        return pl.ds(pl.multiple_of(position * chunk, 8), chunk)

    def exchange(level, position):
        rows = chunk_slice(position)
        return pltpu.make_async_remote_copy(
            src_ref=going.at[level, rows], dst_ref=coming.at[level, rows],
            send_sem=level_send.at[level], recv_sem=level_recv.at[level, position],
            device_id={"leaf": partners[level]}, device_id_type=MESH,
        )

    def result_copies(half, rows):
        return [
            pltpu.make_async_remote_copy(
                src_ref=nested.at[0, 1 - half, rows], dst_ref=nested.at[0, 1 - half, rows],
                send_sem=done_send.at[half, index], recv_sem=done_recv.at[half, index],
                device_id={"blk": peer}, device_id_type=MESH,
            )
            for index, peer in enumerate(peers)
        ]

    def project(value, level):
        high = value.astype(jnp.bfloat16).astype(jnp.float32)
        both = jnp.concatenate([high, value - high], axis=0).astype(jnp.bfloat16)
        product = jnp.dot(both, mats[level], preferred_element_type=jnp.float32)
        return product[:chunk] + product[chunk:]

    def first_level(half, inner):
        for copy in part_copies(half, inner):
            copy.wait_recv()
        start = pl.multiple_of(my_blk * share + inner * chunk, 8)
        value = part[half, pl.ds(start, chunk), :]
        for index in range(blocks - 1):
            value = value + part_in[half, index, chunk_slice(inner), :]
        position = half * per_half + inner
        going[0, chunk_slice(position), :] = project(value, 0)
        exchange(0, position).start()

    def joined(level, position):
        exchange(level, position).wait_recv()
        rows = chunk_slice(position)
        return going[level, rows, :] + coming[level, rows, :]

    def next_level(level, position):
        going[level, chunk_slice(position), :] = project(joined(level - 1, position), level)
        exchange(level, position).start()

    def finish(position):
        half = lax.div(position, per_half)
        start = my_blk * share + lax.rem(position, per_half) * chunk
        rows = pl.ds(pl.multiple_of(start, 8), chunk)
        nested[0, 1 - half, rows, :] = joined(levels - 1, position)
        for copy in result_copies(half, rows):
            copy.start()

    def kernel_tile(source):
        step = min(128, panels)

        def some_rows(index, carry):
            rows = pl.ds(pl.multiple_of(index * step, step), step)
            values = columns[rows, :]
            distance = jnp.zeros((step, panels), jnp.float32)
            for component in range(3):
                gap = geo[component : component + 1, :] - values[:, component : component + 1]
                distance = distance + gap * gap
            soft = distance + 0.5 * (geo[3:4, :] + values[:, 3:4])
            tile[rows, :] = (inv_four_pi * lax.rsqrt(soft)).astype(jnp.bfloat16)
            return carry

        columns[...] = jnp.transpose(source)
        lax.fori_loop(0, panels // step, some_rows, 0)

    def project_part(half, source, barrier=None):
        def some(rows):
            part[half, rows, :] = jnp.dot(
                source[rows, :], sorted_basis[...], preferred_element_type=jnp.float32
            )

        if share % 16 == 0:
            for peer in peers:
                some(pl.ds(pl.multiple_of(peer * share, 16), share))
        else:
            some(pl.ds(0, count))
        if barrier is not None:
            pl.semaphore_wait(barrier, blocks - 1 + levels)
        send_part(half)
        if share % 16 == 0:
            some(pl.ds(pl.multiple_of(my_blk * share, 16), share))

    def send_part(half):
        def one(inner, carry):
            for copy in part_copies(half, inner):
                copy.start()
            return carry

        lax.fori_loop(0, per_half, one, 0)

    def one_step(step):
        @pl.when((step >= per_half) & (step < total))
        def _():
            first_level(1, step - per_half)

        for level in range(1, levels):
            @pl.when((step >= 2 * level) & (step < total + 2 * level))
            def _(level=level):
                next_level(level, step - 2 * level)

        @pl.when((step >= 2 * levels) & (step < total + 2 * levels))
        def _():
            finish(step - 2 * levels)

    early = min(per_half, 5)

    def early_step(step):
        if step < early:
            one_step(step)

    order_load.wait()
    places = lax.broadcasted_iota(jnp.int32, (panels, panels), 0)
    chosen = jnp.where(places == order[...], 1.0, 0.0).astype(jnp.bfloat16)
    basis_load.wait()
    mats_load.start()
    sorted_basis[...] = jnp.dot(
        chosen, basis[...], preferred_element_type=jnp.float32
    ).astype(jnp.bfloat16)
    probe_load.wait()
    project_part(0, probe, barrier)
    for load in geo_loads:
        load.wait()
    scaled[...] = (
        (geo[3:4, :] * probe[...].astype(jnp.float32)).astype(jnp.bfloat16).astype(jnp.float32)
    )
    for copy in geo_copies + scaled_copies:
        copy.start()
    mats_load.wait()
    full_load.start()

    def first_probe(inner, carry):
        first_level(0, inner)
        return carry

    lax.fori_loop(0, per_half, first_probe, 0)
    kernel_tile(geo[...])
    near[...] = jnp.dot(
        scaled[...].astype(jnp.bfloat16), tile[...], preferred_element_type=jnp.float32
    )
    early_step(2)
    for index in range(blocks - 1):
        geo_copies[index].wait_recv()
        kernel_tile(geo_in[index])
        if index == blocks - 2:
            early_step(3)
        scaled_copies[index].wait_recv()
        near[...] += jnp.dot(
            scaled_in[index].astype(jnp.bfloat16), tile[...], preferred_element_type=jnp.float32
        )
    full_load.wait()
    off[...] = (full[...].astype(jnp.float32) - near[...]).astype(jnp.bfloat16)
    early_step(4)
    project_part(1, off)
    lax.fori_loop(early, total + 2 * levels, lambda step, carry: one_step(step), None)
    for level in range(levels):
        pltpu.make_async_remote_copy(
            src_ref=going.at[level], dst_ref=coming.at[level],
            send_sem=level_send.at[level], recv_sem=level_recv.at[level, 0],
            device_id={"leaf": partners[level]}, device_id_type=MESH,
        ).wait_send()
    for half in range(2):
        for copy in result_copies(half, pl.ds(0, share)):
            copy.wait()
        for copy in part_copies(half, None):
            copy.wait_send()
    for copy in geo_copies + scaled_copies:
        copy.wait_send()


def write_out(pieces, off, nested, off_hbm, nested_hbm, sem):
    rows = nested.shape[2] // pieces
    copies = [
        pltpu.make_async_copy(
            nested.at[0, half, pl.ds(piece * rows, rows)],
            nested_hbm.at[0, half, pl.ds(piece * rows, rows)],
            sem.at[half * pieces + piece],
        )
        for half in range(2)
        for piece in range(pieces)
    ]
    copies.append(pltpu.make_async_copy(off, off_hbm, sem.at[2 * pieces]))
    for copy in copies:
        copy.start()
    for copy in copies:
        copy.wait()


def shards(positions, panel_areas, probe_cols, full_sketch, tree_order, leaf_basis, transfer_mats):
    panels = positions.shape[3]
    count = probe_cols.shape[0]
    width = leaf_basis.shape[3]
    levels = transfer_mats.shape[1]
    blocks = lax.axis_size("blk")
    share = count // blocks
    chunk = chunk_rows(share)
    total = 2 * share // chunk
    f32, b16 = jnp.float32, jnp.bfloat16
    dma = pltpu.SemaphoreType.DMA
    whole = pl.BlockSpec(memory_space=pltpu.VMEM)
    hbm = pl.BlockSpec(memory_space=pltpu.HBM)
    offdiag, nested = pl.pallas_call(
        functools.partial(kernel, blocks, levels, chunk),
        out_shape=(
            pltpu.VMEM((count, panels), b16),
            pltpu.VMEM((1, 2, count, width), f32),
        ),
        in_specs=[hbm] * 7,
        out_specs=(whole, whole),
        scratch_shapes=[
            pltpu.VMEM((1, panels), jnp.int32),
            pltpu.VMEM((count, panels), b16),
            pltpu.VMEM((count, panels), b16),
            pltpu.VMEM((panels, width), b16),
            pltpu.VMEM((levels, width, width), b16),
            pltpu.VMEM((panels, width), b16),
            pltpu.VMEM((panels, panels), b16),
            pltpu.VMEM((8, panels), f32),
            pltpu.VMEM((blocks - 1, 8, panels), f32),
            pltpu.VMEM((panels, 8), f32),
            pltpu.VMEM((count, panels), f32),
            pltpu.VMEM((blocks - 1, count, panels), f32),
            pltpu.VMEM((count, panels), f32),
            pltpu.VMEM((2, count, width), f32),
            pltpu.VMEM((2, blocks - 1, share, width), f32),
            pltpu.VMEM((levels, 2 * share, width), f32),
            pltpu.VMEM((levels, 2 * share, width), f32),
            dma((9,)),
            dma((blocks - 1,)), dma((blocks - 1,)),
            dma((blocks - 1,)), dma((blocks - 1,)),
            dma((2, blocks - 1)), dma((2, blocks - 1, total // 2)),
            dma((levels,)), dma((levels, total)),
            dma((2, blocks - 1)), dma((2, blocks - 1)),
        ],
        compiler_params=pltpu.CompilerParams(
            collective_id=0, has_side_effects=True, vmem_limit_bytes=58 * 2**20
        ),
    )(
        positions,
        panel_areas,
        tree_order,
        probe_cols.reshape(count, panels),
        full_sketch.reshape(count, panels),
        leaf_basis.reshape(panels, width),
        transfer_mats.reshape(levels, width, width),
    )
    pieces = 4
    offdiag, nested = pl.pallas_call(
        functools.partial(write_out, pieces),
        out_shape=(
            jax.ShapeDtypeStruct((count, panels), b16),
            jax.ShapeDtypeStruct((1, 2, count, width), f32),
        ),
        in_specs=(whole, whole),
        out_specs=(hbm, hbm),
        scratch_shapes=[dma((1 + 2 * pieces,))],
        compiler_params=pltpu.CompilerParams(vmem_limit_bytes=2**20),
    )(offdiag, nested)
    return (offdiag.reshape(count, 1, 1, panels), nested)


def solution(mesh):
    in_specs = (
        P(None, "leaf", "blk", None),
        P("leaf", "blk", None),
        P(None, "leaf", "blk", None),
        P(None, "leaf", "blk", None),
        P("leaf", "blk", None),
        P("leaf", "blk", None, None),
        P("leaf", None, None, None),
    )
    out_specs = (P(None, "leaf", "blk", None), P("leaf", None, None, None))
    return jax.shard_map(shards, mesh=mesh, in_specs=in_specs, out_specs=out_specs, check_vma=False)
```

```python
import functools
import math

import jax
import jax.numpy as jnp
from jax import lax
from jax.experimental import pallas as pl
from jax.experimental.pallas import tpu as pltpu
from jax.sharding import PartitionSpec as P

MESH = pl.DeviceIdType.MESH
inv_four_pi = 1.0 / (4.0 * math.pi)


def chunk_rows(share):
    return max(rows for rows in range(8, min(share, 32) + 1, 8) if share % rows == 0)


def leaf_partner(me, level):
    step = 2**level
    return me + step * (1 - 2 * lax.rem(lax.div(me, step), 2))


def kernel(
    blocks, levels, chunk,
    pos_hbm, area_hbm, order_hbm, probe_hbm, full_hbm, basis_hbm, mats_hbm,
    off, nested,
    order, probe, full, basis, mats, sorted_basis, tile, geo, geo_in, columns, scaled, scaled_in,
    near, part, part_in, going, coming,
    load_sem, geo_send, geo_recv, scaled_send, scaled_recv, part_send, part_recv,
    level_send, level_recv, done_send, done_recv,
):
    count, panels = probe.shape
    share = count // blocks
    per_half = share // chunk
    lag = 3
    total = 2 * per_half
    my_blk = lax.axis_index("blk")
    my_leaf = lax.axis_index("leaf")
    peers = [lax.rem(my_blk + distance, blocks) for distance in range(1, blocks)]
    partners = [leaf_partner(my_leaf, level) for level in range(levels)]

    loads = [
        pltpu.make_async_copy(source, target, load_sem.at[index])
        for index, (source, target) in enumerate(
            [
                (order_hbm.at[0], order), (basis_hbm, basis), (probe_hbm, probe),
                (area_hbm.at[0], geo.at[pl.ds(3, 1)]),
            ]
            + [(pos_hbm.at[axis, 0], geo.at[pl.ds(axis, 1)]) for axis in range(3)]
            + [(mats_hbm, mats), (full_hbm, full)]
        )
    ]
    order_load, basis_load, probe_load, *geo_loads, mats_load, full_load = loads
    barrier = pltpu.get_barrier_semaphore()
    for peer in peers:
        pl.semaphore_signal(barrier, inc=1, device_id={"blk": peer}, device_id_type=MESH)
    for partner in partners:
        pl.semaphore_signal(barrier, inc=1, device_id={"leaf": partner}, device_id_type=MESH)
    geo[...] = jnp.zeros_like(geo)
    for load in [order_load, basis_load, probe_load] + geo_loads:
        load.start()

    def to_peers(source, target, send, recv):
        return [
            pltpu.make_async_remote_copy(
                src_ref=source, dst_ref=target.at[index], send_sem=send.at[index],
                recv_sem=recv.at[index], device_id={"blk": peer}, device_id_type=MESH,
            )
            for index, peer in enumerate(peers)
        ]

    def part_copies(half, start, size):
        return [
            pltpu.make_async_remote_copy(
                src_ref=part.at[half, pl.ds(pl.multiple_of(peer * share + start, 8), size)],
                dst_ref=part_in.at[half, index, pl.ds(start, size)],
                send_sem=part_send.at[half, index],
                recv_sem=part_recv.at[half, index, min(start, 1)],
                device_id={"blk": peer}, device_id_type=MESH,
            )
            for index, peer in enumerate(peers)
        ]

    geo_copies = to_peers(geo, geo_in, geo_send, geo_recv)
    scaled_copies = to_peers(scaled, scaled_in, scaled_send, scaled_recv)

    def chunk_slice(position):
        return pl.ds(pl.multiple_of(position * chunk, 8), chunk)

    def exchange(level, position):
        rows = chunk_slice(position)
        return pltpu.make_async_remote_copy(
            src_ref=going.at[level, rows], dst_ref=coming.at[level, rows],
            send_sem=level_send.at[level], recv_sem=level_recv.at[level, position],
            device_id={"leaf": partners[level]}, device_id_type=MESH,
        )

    def result_copies(half, rows):
        return [
            pltpu.make_async_remote_copy(
                src_ref=nested.at[0, 1 - half, rows], dst_ref=nested.at[0, 1 - half, rows],
                send_sem=done_send.at[half, index], recv_sem=done_recv.at[half, index],
                device_id={"blk": peer}, device_id_type=MESH,
            )
            for index, peer in enumerate(peers)
        ]

    def project(value, level):
        rows = value.shape[0]
        high = value.astype(jnp.bfloat16).astype(jnp.float32)
        both = jnp.concatenate([high, value - high], axis=0).astype(jnp.bfloat16)
        product = jnp.dot(both, mats[level], preferred_element_type=jnp.float32)
        return product[:rows] + product[rows:]

    def first_level(half, start, size):
        for copy in part_copies(half, start, size):
            copy.wait_recv()
        mine = pl.multiple_of(my_blk * share + start, 8)
        value = part[half, pl.ds(mine, size), :]
        for index in range(blocks - 1):
            value = value + part_in[half, index, pl.ds(start, size), :]
        going[0, pl.ds(half * share + start, size), :] = project(value, 0)

        def send(position, carry):
            exchange(0, position).start()
            return carry

        first = (half * share + start) // chunk
        lax.fori_loop(first, first + size // chunk, send, 0)

    def one_step(step, active):
        for level, on in enumerate(active):
            if on:
                exchange(level, step - lag * level).wait_recv()
        values = [
            going[level, chunk_slice(step - lag * level), :]
            + coming[level, chunk_slice(step - lag * level), :]
            for level in range(levels)
            if active[level]
        ]
        results = [
            project(value, level + 1) if level < levels - 1 else value
            for value, level in zip(values, [level for level in range(levels) if active[level]])
        ]
        for result, level in zip(results, [level for level in range(levels) if active[level]]):
            position = step - lag * level
            if level < levels - 1:
                going[level + 1, chunk_slice(position), :] = result
                exchange(level + 1, position).start()
            else:
                half = lax.div(position, per_half)
                start = my_blk * share + lax.rem(position, per_half) * chunk
                rows = pl.ds(pl.multiple_of(start, 8), chunk)
                nested[0, 1 - half, rows, :] = result
                for copy in result_copies(half, rows):
                    copy.start()

    def steps(start, stop):
        edges = sorted({lag * level for level in range(levels)})
        edges = sorted(set(edges + [edge + total for edge in edges] + [start, stop]))
        for low, high in zip(edges, edges[1:]):
            if low < start or high > stop:
                continue
            active = [lag * level <= low < total + lag * level for level in range(levels)]
            if high - low <= 1:
                one_step(low, active)
            else:

                def body(step, carry, active=active):
                    one_step(step, active)
                    return carry

                lax.fori_loop(low, high, body, 0)

    def kernel_tile(source):
        step = min(128, panels)

        def some_rows(index, carry):
            rows = pl.ds(pl.multiple_of(index * step, step), step)
            values = columns[rows, :]
            distance = jnp.zeros((step, panels), jnp.float32)
            for component in range(3):
                gap = geo[component : component + 1, :] - values[:, component : component + 1]
                distance = distance + gap * gap
            soft = distance + 0.5 * (geo[3:4, :] + values[:, 3:4])
            tile[rows, :] = (inv_four_pi * lax.rsqrt(soft)).astype(jnp.bfloat16)
            return carry

        columns[...] = jnp.transpose(source)
        lax.fori_loop(0, panels // step, some_rows, 0)

    def project_part(half, source, sizes, barrier=None):
        def some(rows):
            part[half, rows, :] = jnp.dot(
                source[rows, :], sorted_basis[...], preferred_element_type=jnp.float32
            )

        if share % 16 == 0:
            for peer in peers:
                some(pl.ds(pl.multiple_of(peer * share, 16), share))
        else:
            some(pl.ds(0, count))
        if barrier is not None:
            pl.semaphore_wait(barrier, blocks - 1 + levels)
        for start, size in sizes:
            for copy in part_copies(half, start, size):
                copy.start()
        if share % 16 == 0:
            some(pl.ds(pl.multiple_of(my_blk * share, 16), share))

    early = min(per_half, 3)
    probe_sizes = [(0, chunk)] + ([(chunk, share - chunk)] if share > chunk else [])

    def early_step(step):
        if step < early:
            steps(step, step + 1)

    order_load.wait()
    places = lax.broadcasted_iota(jnp.int32, (panels, panels), 0)
    chosen = jnp.where(places == order[...], 1.0, 0.0).astype(jnp.bfloat16)
    basis_load.wait()
    mats_load.start()
    sorted_basis[...] = jnp.dot(
        chosen, basis[...], preferred_element_type=jnp.float32
    ).astype(jnp.bfloat16)
    probe_load.wait()
    project_part(0, probe, probe_sizes, barrier)
    for load in geo_loads:
        load.wait()
    scaled[...] = (
        (geo[3:4, :] * probe[...].astype(jnp.float32)).astype(jnp.bfloat16).astype(jnp.float32)
    )
    for copy in geo_copies + scaled_copies:
        copy.start()
    mats_load.wait()
    full_load.start()

    for start, size in probe_sizes:
        first_level(0, start, size)
    kernel_tile(geo[...])
    near[...] = jnp.dot(
        scaled[...].astype(jnp.bfloat16), tile[...], preferred_element_type=jnp.float32
    )
    early_step(0)
    for index in range(blocks - 1):
        geo_copies[index].wait_recv()
        kernel_tile(geo_in[index])
        if index == blocks - 2:
            early_step(1)
        scaled_copies[index].wait_recv()
        near[...] += jnp.dot(
            scaled_in[index].astype(jnp.bfloat16), tile[...], preferred_element_type=jnp.float32
        )
    full_load.wait()
    off[...] = (full[...].astype(jnp.float32) - near[...]).astype(jnp.bfloat16)
    project_part(1, off, [(0, share)])
    early_step(2)
    first_level(1, 0, share)
    steps(early, total + lag * (levels - 1))
    for level in range(levels):
        pltpu.make_async_remote_copy(
            src_ref=going.at[level], dst_ref=coming.at[level],
            send_sem=level_send.at[level], recv_sem=level_recv.at[level, 0],
            device_id={"leaf": partners[level]}, device_id_type=MESH,
        ).wait_send()
    for half in range(2):
        for copy in result_copies(half, pl.ds(0, share)):
            copy.wait()
        for copy in part_copies(half, 0, share):
            copy.wait_send()
    for copy in geo_copies + scaled_copies:
        copy.wait_send()


def write_out(pieces, off, nested, off_hbm, nested_hbm, sem):
    rows = nested.shape[2] // pieces
    copies = [
        pltpu.make_async_copy(
            nested.at[0, half, pl.ds(piece * rows, rows)],
            nested_hbm.at[0, half, pl.ds(piece * rows, rows)],
            sem.at[half * pieces + piece],
        )
        for half in range(2)
        for piece in range(pieces)
    ]
    copies.append(pltpu.make_async_copy(off, off_hbm, sem.at[2 * pieces]))
    for copy in copies:
        copy.start()
    for copy in copies:
        copy.wait()


def shards(positions, panel_areas, probe_cols, full_sketch, tree_order, leaf_basis, transfer_mats):
    panels = positions.shape[3]
    count = probe_cols.shape[0]
    width = leaf_basis.shape[3]
    levels = transfer_mats.shape[1]
    blocks = lax.axis_size("blk")
    share = count // blocks
    chunk = chunk_rows(share)
    total = 2 * share // chunk
    f32, b16 = jnp.float32, jnp.bfloat16
    dma = pltpu.SemaphoreType.DMA
    whole = pl.BlockSpec(memory_space=pltpu.VMEM)
    hbm = pl.BlockSpec(memory_space=pltpu.HBM)
    offdiag, nested = pl.pallas_call(
        functools.partial(kernel, blocks, levels, chunk),
        out_shape=(
            pltpu.VMEM((count, panels), b16),
            pltpu.VMEM((1, 2, count, width), f32),
        ),
        in_specs=[hbm] * 7,
        out_specs=(whole, whole),
        scratch_shapes=[
            pltpu.VMEM((1, panels), jnp.int32),
            pltpu.VMEM((count, panels), b16),
            pltpu.VMEM((count, panels), b16),
            pltpu.VMEM((panels, width), b16),
            pltpu.VMEM((levels, width, width), b16),
            pltpu.VMEM((panels, width), b16),
            pltpu.VMEM((panels, panels), b16),
            pltpu.VMEM((8, panels), f32),
            pltpu.VMEM((blocks - 1, 8, panels), f32),
            pltpu.VMEM((panels, 8), f32),
            pltpu.VMEM((count, panels), f32),
            pltpu.VMEM((blocks - 1, count, panels), f32),
            pltpu.VMEM((count, panels), f32),
            pltpu.VMEM((2, count, width), f32),
            pltpu.VMEM((2, blocks - 1, share, width), f32),
            pltpu.VMEM((levels, 2 * share, width), f32),
            pltpu.VMEM((levels, 2 * share, width), f32),
            dma((9,)),
            dma((blocks - 1,)), dma((blocks - 1,)),
            dma((blocks - 1,)), dma((blocks - 1,)),
            dma((2, blocks - 1)), dma((2, blocks - 1, 2)),
            dma((levels,)), dma((levels, total)),
            dma((2, blocks - 1)), dma((2, blocks - 1)),
        ],
        compiler_params=pltpu.CompilerParams(
            collective_id=0, has_side_effects=True, vmem_limit_bytes=58 * 2**20
        ),
    )(
        positions,
        panel_areas,
        tree_order,
        probe_cols.reshape(count, panels),
        full_sketch.reshape(count, panels),
        leaf_basis.reshape(panels, width),
        transfer_mats.reshape(levels, width, width),
    )
    pieces = 4
    offdiag, nested = pl.pallas_call(
        functools.partial(write_out, pieces),
        out_shape=(
            jax.ShapeDtypeStruct((count, panels), b16),
            jax.ShapeDtypeStruct((1, 2, count, width), f32),
        ),
        in_specs=(whole, whole),
        out_specs=(hbm, hbm),
        scratch_shapes=[dma((1 + 2 * pieces,))],
        compiler_params=pltpu.CompilerParams(vmem_limit_bytes=2**20),
    )(offdiag, nested)
    return (offdiag.reshape(count, 1, 1, panels), nested)


def solution(mesh):
    in_specs = (
        P(None, "leaf", "blk", None),
        P("leaf", "blk", None),
        P(None, "leaf", "blk", None),
        P(None, "leaf", "blk", None),
        P("leaf", "blk", None),
        P("leaf", "blk", None, None),
        P("leaf", None, None, None),
    )
    out_specs = (P(None, "leaf", "blk", None), P("leaf", None, None, None))
    return jax.shard_map(shards, mesh=mesh, in_specs=in_specs, out_specs=out_specs, check_vma=False)
```

```python
import functools
import math

import jax
import jax.numpy as jnp
from jax import lax
from jax.experimental import pallas as pl
from jax.experimental.pallas import tpu as pltpu
from jax.sharding import PartitionSpec as P

MESH = pl.DeviceIdType.MESH
inv_four_pi = 1.0 / (4.0 * math.pi)


def chunk_rows(share):
    return max(rows for rows in range(8, min(share, 32) + 1, 8) if share % rows == 0)


def leaf_partner(me, level):
    step = 2**level
    return me + step * (1 - 2 * lax.rem(lax.div(me, step), 2))


def kernel(
    blocks, levels, chunk,
    pos_hbm, area_hbm, order_hbm, probe_hbm, full_hbm, basis_hbm, mats_hbm,
    off, nested,
    order, probe, full, basis, mats, sorted_basis, tile, geo, geo_in, columns, scaled, scaled_in,
    near, part, part_in, going, coming,
    load_sem, geo_send, geo_recv, scaled_send, scaled_recv, part_send, part_recv,
    level_send, level_recv, done_send, done_recv,
):
    count, panels = probe.shape
    share = count // blocks
    per_half = share // chunk
    lag = 3
    total = 2 * per_half
    my_blk = lax.axis_index("blk")
    my_leaf = lax.axis_index("leaf")
    peers = [lax.rem(my_blk + distance, blocks) for distance in range(1, blocks)]
    partners = [leaf_partner(my_leaf, level) for level in range(levels)]

    loads = [
        pltpu.make_async_copy(source, target, load_sem.at[index])
        for index, (source, target) in enumerate(
            [
                (order_hbm.at[0], order), (basis_hbm, basis), (probe_hbm, probe),
                (area_hbm.at[0], geo.at[pl.ds(3, 1)]),
            ]
            + [(pos_hbm.at[axis, 0], geo.at[pl.ds(axis, 1)]) for axis in range(3)]
            + [(mats_hbm, mats), (full_hbm, full)]
        )
    ]
    order_load, basis_load, probe_load, *geo_loads, mats_load, full_load = loads
    barrier = pltpu.get_barrier_semaphore()
    for peer in peers:
        pl.semaphore_signal(barrier, inc=1, device_id={"blk": peer}, device_id_type=MESH)
    for partner in partners:
        pl.semaphore_signal(barrier, inc=1, device_id={"leaf": partner}, device_id_type=MESH)
    geo[...] = jnp.zeros_like(geo)
    for load in [order_load, basis_load, probe_load] + geo_loads:
        load.start()

    def to_peers(source, target, send, recv):
        return [
            pltpu.make_async_remote_copy(
                src_ref=source, dst_ref=target.at[index], send_sem=send.at[index],
                recv_sem=recv.at[index], device_id={"blk": peer}, device_id_type=MESH,
            )
            for index, peer in enumerate(peers)
        ]

    def part_copies(half, start, size, place=0):
        return [
            pltpu.make_async_remote_copy(
                src_ref=part.at[half, pl.ds(pl.multiple_of(peer * share + start, 8), size)],
                dst_ref=part_in.at[half, index, pl.ds(start, size)],
                send_sem=part_send.at[half, index],
                recv_sem=part_recv.at[half, index, place],
                device_id={"blk": peer}, device_id_type=MESH,
            )
            for index, peer in enumerate(peers)
        ]

    geo_copies = to_peers(geo, geo_in, geo_send, geo_recv)
    scaled_copies = to_peers(scaled, scaled_in, scaled_send, scaled_recv)

    def chunk_slice(position):
        return pl.ds(pl.multiple_of(position * chunk, 8), chunk)

    def exchange(level, position):
        rows = chunk_slice(position)
        return pltpu.make_async_remote_copy(
            src_ref=going.at[level, rows], dst_ref=coming.at[level, rows],
            send_sem=level_send.at[level], recv_sem=level_recv.at[level, position],
            device_id={"leaf": partners[level]}, device_id_type=MESH,
        )

    def result_copies(half, rows):
        return [
            pltpu.make_async_remote_copy(
                src_ref=nested.at[0, 1 - half, rows], dst_ref=nested.at[0, 1 - half, rows],
                send_sem=done_send.at[half, index], recv_sem=done_recv.at[half, index],
                device_id={"blk": peer}, device_id_type=MESH,
            )
            for index, peer in enumerate(peers)
        ]

    def project(value, level):
        rows = value.shape[0]
        high = value.astype(jnp.bfloat16).astype(jnp.float32)
        both = jnp.concatenate([high, value - high], axis=0).astype(jnp.bfloat16)
        product = jnp.dot(both, mats[level], preferred_element_type=jnp.float32)
        return product[:rows] + product[rows:]

    def first_level(half, start, size, place):
        for copy in part_copies(half, start, size, place):
            copy.wait_recv()
        mine = pl.multiple_of(my_blk * share + start, 8)
        value = part[half, pl.ds(mine, size), :]
        for index in range(blocks - 1):
            value = value + part_in[half, index, pl.ds(start, size), :]
        going[0, pl.ds(half * share + start, size), :] = project(value, 0)

        def send(position, carry):
            exchange(0, position).start()
            return carry

        first = (half * share + start) // chunk
        lax.fori_loop(first, first + size // chunk, send, 0)

    def one_step(step, active):
        for level, on in enumerate(active):
            if on:
                exchange(level, step - lag * level).wait_recv()
        values = [
            going[level, chunk_slice(step - lag * level), :]
            + coming[level, chunk_slice(step - lag * level), :]
            for level in range(levels)
            if active[level]
        ]
        results = [
            project(value, level + 1) if level < levels - 1 else value
            for value, level in zip(values, [level for level in range(levels) if active[level]])
        ]
        for result, level in zip(results, [level for level in range(levels) if active[level]]):
            position = step - lag * level
            if level < levels - 1:
                going[level + 1, chunk_slice(position), :] = result
                exchange(level + 1, position).start()
            else:
                half = lax.div(position, per_half)
                start = my_blk * share + lax.rem(position, per_half) * chunk
                rows = pl.ds(pl.multiple_of(start, 8), chunk)
                nested[0, 1 - half, rows, :] = result
                for copy in result_copies(half, rows):
                    copy.start()

    def steps(start, stop):
        edges = sorted({lag * level for level in range(levels)})
        edges = sorted(set(edges + [edge + total for edge in edges] + [start, stop]))
        for low, high in zip(edges, edges[1:]):
            if low < start or high > stop:
                continue
            active = [lag * level <= low < total + lag * level for level in range(levels)]
            if high - low <= 1:
                one_step(low, active)
            else:

                def body(step, carry, active=active):
                    one_step(step, active)
                    return carry

                lax.fori_loop(low, high, body, 0)

    def kernel_tile(source):
        step = min(128, panels)

        def some_rows(index, carry):
            rows = pl.ds(pl.multiple_of(index * step, step), step)
            values = columns[rows, :]
            distance = jnp.zeros((step, panels), jnp.float32)
            for component in range(3):
                gap = geo[component : component + 1, :] - values[:, component : component + 1]
                distance = distance + gap * gap
            soft = distance + 0.5 * (geo[3:4, :] + values[:, 3:4])
            tile[rows, :] = (inv_four_pi * lax.rsqrt(soft)).astype(jnp.bfloat16)
            return carry

        columns[...] = jnp.transpose(source)
        lax.fori_loop(0, panels // step, some_rows, 0)

    def project_part(half, source, sizes, barrier=None):
        def some(rows):
            part[half, rows, :] = jnp.dot(
                source[rows, :], sorted_basis[...], preferred_element_type=jnp.float32
            )

        if share % 16 == 0:
            for peer in peers:
                some(pl.ds(pl.multiple_of(peer * share, 16), share))
        else:
            some(pl.ds(0, count))
        if barrier is not None:
            pl.semaphore_wait(barrier, blocks - 1 + levels)
        for piece in sizes:
            for copy in part_copies(half, *piece):
                copy.start()
        if share % 16 == 0:
            some(pl.ds(pl.multiple_of(my_blk * share, 16), share))

    early = min(per_half, 3)

    def pieces(chunks):
        found, start = [], 0
        for size in [rows * chunk for rows in chunks] + [share]:
            size = min(size, share - start)
            if size > 0:
                found.append((start, size, len(found)))
                start += size
        return found

    probe_sizes, sketch_sizes = pieces([1, 2, 3]), pieces([3])

    def early_step(step):
        if step < early:
            steps(step, step + 1)

    order_load.wait()
    places = lax.broadcasted_iota(jnp.int32, (panels, panels), 0)
    chosen = jnp.where(places == order[...], 1.0, 0.0).astype(jnp.bfloat16)
    basis_load.wait()
    mats_load.start()
    sorted_basis[...] = jnp.dot(
        chosen, basis[...], preferred_element_type=jnp.float32
    ).astype(jnp.bfloat16)
    probe_load.wait()
    project_part(0, probe, probe_sizes, barrier)
    for load in geo_loads:
        load.wait()
    scaled[...] = (
        (geo[3:4, :] * probe[...].astype(jnp.float32)).astype(jnp.bfloat16).astype(jnp.float32)
    )
    for copy in geo_copies + scaled_copies:
        copy.start()
    mats_load.wait()
    full_load.start()

    for piece in probe_sizes:
        first_level(0, *piece)
    kernel_tile(geo[...])
    near[...] = jnp.dot(
        scaled[...].astype(jnp.bfloat16), tile[...], preferred_element_type=jnp.float32
    )
    early_step(0)
    for index in range(blocks - 1):
        geo_copies[index].wait_recv()
        kernel_tile(geo_in[index])
        if index == blocks - 2:
            early_step(1)
        scaled_copies[index].wait_recv()
        near[...] += jnp.dot(
            scaled_in[index].astype(jnp.bfloat16), tile[...], preferred_element_type=jnp.float32
        )
    full_load.wait()
    off[...] = (full[...].astype(jnp.float32) - near[...]).astype(jnp.bfloat16)
    project_part(1, off, sketch_sizes)
    early_step(2)
    for piece in sketch_sizes:
        first_level(1, *piece)
    steps(early, total + lag * (levels - 1))
    for level in range(levels):
        pltpu.make_async_remote_copy(
            src_ref=going.at[level], dst_ref=coming.at[level],
            send_sem=level_send.at[level], recv_sem=level_recv.at[level, 0],
            device_id={"leaf": partners[level]}, device_id_type=MESH,
        ).wait_send()
    for half in range(2):
        for copy in result_copies(half, pl.ds(0, share)):
            copy.wait()
        for copy in part_copies(half, 0, share):
            copy.wait_send()
    for copy in geo_copies + scaled_copies:
        copy.wait_send()


def write_out(pieces, off, nested, off_hbm, nested_hbm, sem):
    rows = nested.shape[2] // pieces
    copies = [
        pltpu.make_async_copy(
            nested.at[0, half, pl.ds(piece * rows, rows)],
            nested_hbm.at[0, half, pl.ds(piece * rows, rows)],
            sem.at[half * pieces + piece],
        )
        for half in range(2)
        for piece in range(pieces)
    ]
    copies.append(pltpu.make_async_copy(off, off_hbm, sem.at[2 * pieces]))
    for copy in copies:
        copy.start()
    for copy in copies:
        copy.wait()


def shards(positions, panel_areas, probe_cols, full_sketch, tree_order, leaf_basis, transfer_mats):
    panels = positions.shape[3]
    count = probe_cols.shape[0]
    width = leaf_basis.shape[3]
    levels = transfer_mats.shape[1]
    blocks = lax.axis_size("blk")
    share = count // blocks
    chunk = chunk_rows(share)
    total = 2 * share // chunk
    f32, b16 = jnp.float32, jnp.bfloat16
    dma = pltpu.SemaphoreType.DMA
    whole = pl.BlockSpec(memory_space=pltpu.VMEM)
    hbm = pl.BlockSpec(memory_space=pltpu.HBM)
    offdiag, nested = pl.pallas_call(
        functools.partial(kernel, blocks, levels, chunk),
        out_shape=(
            pltpu.VMEM((count, panels), b16),
            pltpu.VMEM((1, 2, count, width), f32),
        ),
        in_specs=[hbm] * 7,
        out_specs=(whole, whole),
        scratch_shapes=[
            pltpu.VMEM((1, panels), jnp.int32),
            pltpu.VMEM((count, panels), b16),
            pltpu.VMEM((count, panels), b16),
            pltpu.VMEM((panels, width), b16),
            pltpu.VMEM((levels, width, width), b16),
            pltpu.VMEM((panels, width), b16),
            pltpu.VMEM((panels, panels), b16),
            pltpu.VMEM((8, panels), f32),
            pltpu.VMEM((blocks - 1, 8, panels), f32),
            pltpu.VMEM((panels, 8), f32),
            pltpu.VMEM((count, panels), f32),
            pltpu.VMEM((blocks - 1, count, panels), f32),
            pltpu.VMEM((count, panels), f32),
            pltpu.VMEM((2, count, width), f32),
            pltpu.VMEM((2, blocks - 1, share, width), f32),
            pltpu.VMEM((levels, 2 * share, width), f32),
            pltpu.VMEM((levels, 2 * share, width), f32),
            dma((9,)),
            dma((blocks - 1,)), dma((blocks - 1,)),
            dma((blocks - 1,)), dma((blocks - 1,)),
            dma((2, blocks - 1)), dma((2, blocks - 1, 4)),
            dma((levels,)), dma((levels, total)),
            dma((2, blocks - 1)), dma((2, blocks - 1)),
        ],
        compiler_params=pltpu.CompilerParams(
            collective_id=0, has_side_effects=True, vmem_limit_bytes=58 * 2**20
        ),
    )(
        positions,
        panel_areas,
        tree_order,
        probe_cols.reshape(count, panels),
        full_sketch.reshape(count, panels),
        leaf_basis.reshape(panels, width),
        transfer_mats.reshape(levels, width, width),
    )
    pieces = 4
    offdiag, nested = pl.pallas_call(
        functools.partial(write_out, pieces),
        out_shape=(
            jax.ShapeDtypeStruct((count, panels), b16),
            jax.ShapeDtypeStruct((1, 2, count, width), f32),
        ),
        in_specs=(whole, whole),
        out_specs=(hbm, hbm),
        scratch_shapes=[dma((1 + 2 * pieces,))],
        compiler_params=pltpu.CompilerParams(vmem_limit_bytes=2**20),
    )(offdiag, nested)
    return (offdiag.reshape(count, 1, 1, panels), nested)


def solution(mesh):
    in_specs = (
        P(None, "leaf", "blk", None),
        P("leaf", "blk", None),
        P(None, "leaf", "blk", None),
        P(None, "leaf", "blk", None),
        P("leaf", "blk", None),
        P("leaf", "blk", None, None),
        P("leaf", None, None, None),
    )
    out_specs = (P(None, "leaf", "blk", None), P("leaf", None, None, None))
    return jax.shard_map(shards, mesh=mesh, in_specs=in_specs, out_specs=out_specs, check_vma=False)
```

```python
import functools
import math

import jax
import jax.numpy as jnp
from jax import lax
from jax.experimental import pallas as pl
from jax.experimental.pallas import tpu as pltpu
from jax.sharding import PartitionSpec as P

MESH = pl.DeviceIdType.MESH
inv_four_pi = 1.0 / (4.0 * math.pi)


def chunk_rows(share):
    return max(rows for rows in range(8, min(share, 32) + 1, 8) if share % rows == 0)


def leaf_partner(me, level):
    step = 2**level
    return me + step * (1 - 2 * lax.rem(lax.div(me, step), 2))


def kernel(
    blocks, levels, chunk,
    pos_hbm, area_hbm, order_hbm, probe_hbm, full_hbm, basis_hbm, mats_hbm,
    off, nested,
    order, probe, full, basis, mats, sorted_basis, tile, geo, geo_in, columns, scaled, scaled_in,
    near, part, part_in, going, coming,
    load_sem, geo_send, geo_recv, scaled_send, scaled_recv, part_send, part_recv,
    level_send, level_recv, done_send, done_recv,
):
    count, panels = probe.shape
    share = count // blocks
    per_half = share // chunk
    lag = 3
    total = 2 * per_half
    my_blk = lax.axis_index("blk")
    my_leaf = lax.axis_index("leaf")
    peers = [lax.rem(my_blk + distance, blocks) for distance in range(1, blocks)]
    partners = [leaf_partner(my_leaf, level) for level in range(levels)]

    loads = [
        pltpu.make_async_copy(source, target, load_sem.at[index])
        for index, (source, target) in enumerate(
            [
                (order_hbm.at[0], order), (basis_hbm, basis), (probe_hbm, probe),
                (area_hbm.at[0], geo.at[pl.ds(3, 1)]),
            ]
            + [(pos_hbm.at[axis, 0], geo.at[pl.ds(axis, 1)]) for axis in range(3)]
            + [(mats_hbm, mats), (full_hbm, full)]
        )
    ]
    order_load, basis_load, probe_load, *geo_loads, mats_load, full_load = loads
    barrier = pltpu.get_barrier_semaphore()
    for peer in peers:
        pl.semaphore_signal(barrier, inc=1, device_id={"blk": peer}, device_id_type=MESH)
    for partner in partners:
        pl.semaphore_signal(barrier, inc=1, device_id={"leaf": partner}, device_id_type=MESH)
    geo[...] = jnp.zeros_like(geo)
    for load in [order_load, basis_load, probe_load] + geo_loads:
        load.start()

    def to_peers(source, target, send, recv):
        return [
            pltpu.make_async_remote_copy(
                src_ref=source, dst_ref=target.at[index], send_sem=send.at[index],
                recv_sem=recv.at[index], device_id={"blk": peer}, device_id_type=MESH,
            )
            for index, peer in enumerate(peers)
        ]

    def part_copies(half, start, size, place=0):
        return [
            pltpu.make_async_remote_copy(
                src_ref=part.at[half, pl.ds(pl.multiple_of(peer * share + start, 8), size)],
                dst_ref=part_in.at[half, index, pl.ds(start, size)],
                send_sem=part_send.at[half, index],
                recv_sem=part_recv.at[half, index, place],
                device_id={"blk": peer}, device_id_type=MESH,
            )
            for index, peer in enumerate(peers)
        ]

    geo_copies = to_peers(geo, geo_in, geo_send, geo_recv)
    scaled_copies = to_peers(scaled, scaled_in, scaled_send, scaled_recv)

    def chunk_slice(position):
        return pl.ds(pl.multiple_of(position * chunk, 8), chunk)

    def exchange(level, position):
        rows = chunk_slice(position)
        return pltpu.make_async_remote_copy(
            src_ref=going.at[level, rows], dst_ref=coming.at[level, rows],
            send_sem=level_send.at[level], recv_sem=level_recv.at[level, position],
            device_id={"leaf": partners[level]}, device_id_type=MESH,
        )

    def result_copies(half, rows):
        return [
            pltpu.make_async_remote_copy(
                src_ref=nested.at[0, 1 - half, rows], dst_ref=nested.at[0, 1 - half, rows],
                send_sem=done_send.at[half, index], recv_sem=done_recv.at[half, index],
                device_id={"blk": peer}, device_id_type=MESH,
            )
            for index, peer in enumerate(peers)
        ]

    def project(value, level):
        rows = value.shape[0]
        high = value.astype(jnp.bfloat16).astype(jnp.float32)
        both = jnp.concatenate([high, value - high], axis=0).astype(jnp.bfloat16)
        product = jnp.dot(both, mats[level], preferred_element_type=jnp.float32)
        return product[:rows] + product[rows:]

    def first_level(half, start, size, place):
        for copy in part_copies(half, start, size, place):
            copy.wait_recv()
        mine = pl.multiple_of(my_blk * share + start, 8)
        value = part[half, pl.ds(mine, size), :]
        for index in range(blocks - 1):
            value = value + part_in[half, index, pl.ds(start, size), :]
        going[0, pl.ds(half * share + start, size), :] = project(value, 0)

        def send(position, carry):
            exchange(0, position).start()
            return carry

        first = (half * share + start) // chunk
        lax.fori_loop(first, first + size // chunk, send, 0)

    def one_step(step, active):
        for level, on in enumerate(active):
            if on:
                exchange(level, step - lag * level).wait_recv()
        values = [
            going[level, chunk_slice(step - lag * level), :]
            + coming[level, chunk_slice(step - lag * level), :]
            for level in range(levels)
            if active[level]
        ]
        results = [
            project(value, level + 1) if level < levels - 1 else value
            for value, level in zip(values, [level for level in range(levels) if active[level]])
        ]
        for result, level in zip(results, [level for level in range(levels) if active[level]]):
            position = step - lag * level
            if level < levels - 1:
                going[level + 1, chunk_slice(position), :] = result
                exchange(level + 1, position).start()
            else:
                half = lax.div(position, per_half)
                start = my_blk * share + lax.rem(position, per_half) * chunk
                rows = pl.ds(pl.multiple_of(start, 8), chunk)
                nested[0, 1 - half, rows, :] = result
                for copy in result_copies(half, rows):
                    copy.start()

    def steps(start, stop):
        edges = sorted({lag * level for level in range(levels)})
        edges = sorted(set(edges + [edge + total for edge in edges] + [start, stop]))
        for low, high in zip(edges, edges[1:]):
            if low < start or high > stop:
                continue
            active = [lag * level <= low < total + lag * level for level in range(levels)]
            if high - low <= 1:
                one_step(low, active)
            else:

                def body(step, carry, active=active):
                    one_step(step, active)
                    return carry

                lax.fori_loop(low, high, body, 0)

    def kernel_tile(source):
        step = min(128, panels)

        def some_rows(index, carry):
            rows = pl.ds(pl.multiple_of(index * step, step), step)
            values = columns[rows, :]
            distance = jnp.zeros((step, panels), jnp.float32)
            for component in range(3):
                gap = geo[component : component + 1, :] - values[:, component : component + 1]
                distance = distance + gap * gap
            soft = distance + 0.5 * (geo[3:4, :] + values[:, 3:4])
            tile[rows, :] = (inv_four_pi * lax.rsqrt(soft)).astype(jnp.bfloat16)
            return carry

        columns[...] = jnp.transpose(source)
        lax.fori_loop(0, panels // step, some_rows, 0)

    def project_part(half, source, sizes, barrier=None):
        def some(rows):
            part[half, rows, :] = jnp.dot(
                source[rows, :], sorted_basis[...], preferred_element_type=jnp.float32
            )

        if share % 16 == 0:
            for peer in peers:
                some(pl.ds(pl.multiple_of(peer * share, 16), share))
        else:
            some(pl.ds(0, count))
        if barrier is not None:
            pl.semaphore_wait(barrier, blocks - 1 + levels)
        for piece in sizes:
            for copy in part_copies(half, *piece):
                copy.start()
        if share % 16 == 0:
            some(pl.ds(pl.multiple_of(my_blk * share, 16), share))

    def pieces(chunks):
        found, start = [], 0
        for size in [rows * chunk for rows in chunks] + [share]:
            size = min(size, share - start)
            if size > 0:
                found.append((start, size, len(found)))
                start += size
        return found

    probe_sizes, sketch_sizes = pieces([1, 2, 3]), pieces([3])

    order_load.wait()
    places = lax.broadcasted_iota(jnp.int32, (panels, panels), 0)
    chosen = jnp.where(places == order[...], 1.0, 0.0).astype(jnp.bfloat16)
    basis_load.wait()
    mats_load.start()
    sorted_basis[...] = jnp.dot(
        chosen, basis[...], preferred_element_type=jnp.float32
    ).astype(jnp.bfloat16)
    probe_load.wait()
    project_part(0, probe, probe_sizes, barrier)
    for load in geo_loads:
        load.wait()
    scaled[...] = (
        (geo[3:4, :] * probe[...].astype(jnp.float32)).astype(jnp.bfloat16).astype(jnp.float32)
    )
    for copy in geo_copies + scaled_copies:
        copy.start()
    mats_load.wait()
    full_load.start()

    for piece in probe_sizes:
        first_level(0, *piece)
    def own_near():
        near[...] = jnp.dot(
            scaled[...].astype(jnp.bfloat16), tile[...], preferred_element_type=jnp.float32
        )

    def peer_tile(index):
        geo_copies[index].wait_recv()
        kernel_tile(geo_in[index])

    def peer_near(index):
        scaled_copies[index].wait_recv()
        near[...] += jnp.dot(
            scaled_in[index].astype(jnp.bfloat16), tile[...], preferred_element_type=jnp.float32
        )
        if index == blocks - 2:
            full_load.wait()
            off[...] = (full[...].astype(jnp.float32) - near[...]).astype(jnp.bfloat16)

    tasks = [lambda: kernel_tile(geo[...]), own_near]
    for index in range(blocks - 1):
        tasks += [functools.partial(peer_tile, index), functools.partial(peer_near, index)]
    tasks.append(lambda: project_part(1, off, sketch_sizes))
    tasks += [functools.partial(first_level, 1, *piece) for piece in sketch_sizes]
    early = min(len(tasks) - 1, per_half)
    for step, task in enumerate(tasks):
        task()
        if step < early:
            steps(step, step + 1)
    steps(early, total + lag * (levels - 1))
    for level in range(levels):
        pltpu.make_async_remote_copy(
            src_ref=going.at[level], dst_ref=coming.at[level],
            send_sem=level_send.at[level], recv_sem=level_recv.at[level, 0],
            device_id={"leaf": partners[level]}, device_id_type=MESH,
        ).wait_send()
    for half in range(2):
        for copy in result_copies(half, pl.ds(0, share)):
            copy.wait()
        for copy in part_copies(half, 0, share):
            copy.wait_send()
    for copy in geo_copies + scaled_copies:
        copy.wait_send()


def write_out(pieces, off, nested, off_hbm, nested_hbm, sem):
    rows = nested.shape[2] // pieces
    copies = [
        pltpu.make_async_copy(
            nested.at[0, half, pl.ds(piece * rows, rows)],
            nested_hbm.at[0, half, pl.ds(piece * rows, rows)],
            sem.at[half * pieces + piece],
        )
        for half in range(2)
        for piece in range(pieces)
    ]
    copies.append(pltpu.make_async_copy(off, off_hbm, sem.at[2 * pieces]))
    for copy in copies:
        copy.start()
    for copy in copies:
        copy.wait()


def shards(positions, panel_areas, probe_cols, full_sketch, tree_order, leaf_basis, transfer_mats):
    panels = positions.shape[3]
    count = probe_cols.shape[0]
    width = leaf_basis.shape[3]
    levels = transfer_mats.shape[1]
    blocks = lax.axis_size("blk")
    share = count // blocks
    chunk = chunk_rows(share)
    total = 2 * share // chunk
    f32, b16 = jnp.float32, jnp.bfloat16
    dma = pltpu.SemaphoreType.DMA
    whole = pl.BlockSpec(memory_space=pltpu.VMEM)
    hbm = pl.BlockSpec(memory_space=pltpu.HBM)
    offdiag, nested = pl.pallas_call(
        functools.partial(kernel, blocks, levels, chunk),
        out_shape=(
            pltpu.VMEM((count, panels), b16),
            pltpu.VMEM((1, 2, count, width), f32),
        ),
        in_specs=[hbm] * 7,
        out_specs=(whole, whole),
        scratch_shapes=[
            pltpu.VMEM((1, panels), jnp.int32),
            pltpu.VMEM((count, panels), b16),
            pltpu.VMEM((count, panels), b16),
            pltpu.VMEM((panels, width), b16),
            pltpu.VMEM((levels, width, width), b16),
            pltpu.VMEM((panels, width), b16),
            pltpu.VMEM((panels, panels), b16),
            pltpu.VMEM((8, panels), f32),
            pltpu.VMEM((blocks - 1, 8, panels), f32),
            pltpu.VMEM((panels, 8), f32),
            pltpu.VMEM((count, panels), f32),
            pltpu.VMEM((blocks - 1, count, panels), f32),
            pltpu.VMEM((count, panels), f32),
            pltpu.VMEM((2, count, width), f32),
            pltpu.VMEM((2, blocks - 1, share, width), f32),
            pltpu.VMEM((levels, 2 * share, width), f32),
            pltpu.VMEM((levels, 2 * share, width), f32),
            dma((9,)),
            dma((blocks - 1,)), dma((blocks - 1,)),
            dma((blocks - 1,)), dma((blocks - 1,)),
            dma((2, blocks - 1)), dma((2, blocks - 1, 4)),
            dma((levels,)), dma((levels, total)),
            dma((2, blocks - 1)), dma((2, blocks - 1)),
        ],
        compiler_params=pltpu.CompilerParams(
            collective_id=0, has_side_effects=True, vmem_limit_bytes=58 * 2**20
        ),
    )(
        positions,
        panel_areas,
        tree_order,
        probe_cols.reshape(count, panels),
        full_sketch.reshape(count, panels),
        leaf_basis.reshape(panels, width),
        transfer_mats.reshape(levels, width, width),
    )
    pieces = 4
    offdiag, nested = pl.pallas_call(
        functools.partial(write_out, pieces),
        out_shape=(
            jax.ShapeDtypeStruct((count, panels), b16),
            jax.ShapeDtypeStruct((1, 2, count, width), f32),
        ),
        in_specs=(whole, whole),
        out_specs=(hbm, hbm),
        scratch_shapes=[dma((1 + 2 * pieces,))],
        compiler_params=pltpu.CompilerParams(vmem_limit_bytes=2**20),
    )(offdiag, nested)
    return (offdiag.reshape(count, 1, 1, panels), nested)


def solution(mesh):
    in_specs = (
        P(None, "leaf", "blk", None),
        P("leaf", "blk", None),
        P(None, "leaf", "blk", None),
        P(None, "leaf", "blk", None),
        P("leaf", "blk", None),
        P("leaf", "blk", None, None),
        P("leaf", None, None, None),
    )
    out_specs = (P(None, "leaf", "blk", None), P("leaf", None, None, None))
    return jax.shard_map(shards, mesh=mesh, in_specs=in_specs, out_specs=out_specs, check_vma=False)
```

```python
import functools
import math

import jax
import jax.numpy as jnp
from jax import lax
from jax.experimental import pallas as pl
from jax.experimental.pallas import tpu as pltpu
from jax.sharding import PartitionSpec as P

MESH = pl.DeviceIdType.MESH
inv_four_pi = 1.0 / (4.0 * math.pi)


def chunk_rows(share):
    return max(rows for rows in range(8, min(share, 48) + 1, 8) if share % rows == 0)


def leaf_partner(me, level):
    step = 2**level
    return me + step * (1 - 2 * lax.rem(lax.div(me, step), 2))


def kernel(
    blocks, levels, chunk,
    pos_hbm, area_hbm, order_hbm, probe_hbm, full_hbm, basis_hbm, mats_hbm,
    off, nested,
    order, probe, full, basis, mats, sorted_basis, tile, geo, geo_in, columns, scaled, scaled_in,
    near, part, part_in, going, coming,
    load_sem, geo_send, geo_recv, scaled_send, scaled_recv, part_send, part_recv,
    level_send, level_recv, done_send, done_recv,
):
    count, panels = probe.shape
    share = count // blocks
    per_half = share // chunk
    lag = 2
    total = 2 * per_half
    my_blk = lax.axis_index("blk")
    my_leaf = lax.axis_index("leaf")
    peers = [lax.rem(my_blk + distance, blocks) for distance in range(1, blocks)]
    partners = [leaf_partner(my_leaf, level) for level in range(levels)]

    loads = [
        pltpu.make_async_copy(source, target, load_sem.at[index])
        for index, (source, target) in enumerate(
            [
                (order_hbm.at[0], order), (basis_hbm, basis), (probe_hbm, probe),
                (area_hbm.at[0], geo.at[pl.ds(3, 1)]),
            ]
            + [(pos_hbm.at[axis, 0], geo.at[pl.ds(axis, 1)]) for axis in range(3)]
            + [(mats_hbm, mats), (full_hbm, full)]
        )
    ]
    order_load, basis_load, probe_load, *geo_loads, mats_load, full_load = loads
    barrier = pltpu.get_barrier_semaphore()
    for peer in peers:
        pl.semaphore_signal(barrier, inc=1, device_id={"blk": peer}, device_id_type=MESH)
    for partner in partners:
        pl.semaphore_signal(barrier, inc=1, device_id={"leaf": partner}, device_id_type=MESH)
    geo[...] = jnp.zeros_like(geo)
    for load in [order_load, basis_load, probe_load] + geo_loads:
        load.start()

    def to_peers(source, target, send, recv):
        return [
            pltpu.make_async_remote_copy(
                src_ref=source, dst_ref=target.at[index], send_sem=send.at[index],
                recv_sem=recv.at[index], device_id={"blk": peer}, device_id_type=MESH,
            )
            for index, peer in enumerate(peers)
        ]

    def part_copies(half, start, size, place=0):
        return [
            pltpu.make_async_remote_copy(
                src_ref=part.at[half, pl.ds(pl.multiple_of(peer * share + start, 8), size)],
                dst_ref=part_in.at[half, index, pl.ds(start, size)],
                send_sem=part_send.at[half, index],
                recv_sem=part_recv.at[half, index, place],
                device_id={"blk": peer}, device_id_type=MESH,
            )
            for index, peer in enumerate(peers)
        ]

    geo_copies = to_peers(geo, geo_in, geo_send, geo_recv)
    scaled_copies = to_peers(scaled, scaled_in, scaled_send, scaled_recv)

    def chunk_slice(position):
        return pl.ds(pl.multiple_of(position * chunk, 8), chunk)

    def exchange(level, position):
        rows = chunk_slice(position)
        return pltpu.make_async_remote_copy(
            src_ref=going.at[level, rows], dst_ref=coming.at[level, rows],
            send_sem=level_send.at[level], recv_sem=level_recv.at[level, position],
            device_id={"leaf": partners[level]}, device_id_type=MESH,
        )

    def result_copies(half, rows):
        return [
            pltpu.make_async_remote_copy(
                src_ref=nested.at[0, 1 - half, rows], dst_ref=nested.at[0, 1 - half, rows],
                send_sem=done_send.at[half, index], recv_sem=done_recv.at[half, index],
                device_id={"blk": peer}, device_id_type=MESH,
            )
            for index, peer in enumerate(peers)
        ]

    def project(value, level):
        rows = value.shape[0]
        high = value.astype(jnp.bfloat16).astype(jnp.float32)
        both = jnp.concatenate([high, value - high], axis=0).astype(jnp.bfloat16)
        product = jnp.dot(both, mats[level], preferred_element_type=jnp.float32)
        return product[:rows] + product[rows:]

    def first_level(half, start, size, place):
        for copy in part_copies(half, start, size, place):
            copy.wait_recv()
        mine = pl.multiple_of(my_blk * share + start, 8)
        value = part[half, pl.ds(mine, size), :]
        for index in range(blocks - 1):
            value = value + part_in[half, index, pl.ds(start, size), :]
        going[0, pl.ds(half * share + start, size), :] = project(value, 0)

        def send(position, carry):
            exchange(0, position).start()
            return carry

        first = (half * share + start) // chunk
        lax.fori_loop(first, first + size // chunk, send, 0)

    def one_step(step, active):
        for level, on in enumerate(active):
            if on:
                exchange(level, step - lag * level).wait_recv()
        values = [
            going[level, chunk_slice(step - lag * level), :]
            + coming[level, chunk_slice(step - lag * level), :]
            for level in range(levels)
            if active[level]
        ]
        results = [
            project(value, level + 1) if level < levels - 1 else value
            for value, level in zip(values, [level for level in range(levels) if active[level]])
        ]
        for result, level in zip(results, [level for level in range(levels) if active[level]]):
            position = step - lag * level
            if level < levels - 1:
                going[level + 1, chunk_slice(position), :] = result
                exchange(level + 1, position).start()
            else:
                half = lax.div(position, per_half)
                start = my_blk * share + lax.rem(position, per_half) * chunk
                rows = pl.ds(pl.multiple_of(start, 8), chunk)
                nested[0, 1 - half, rows, :] = result
                for copy in result_copies(half, rows):
                    copy.start()

    def steps(start, stop):
        edges = sorted({lag * level for level in range(levels)})
        edges = sorted(set(edges + [edge + total for edge in edges] + [start, stop]))
        for low, high in zip(edges, edges[1:]):
            if low < start or high > stop:
                continue
            active = [lag * level <= low < total + lag * level for level in range(levels)]
            if high - low <= 1:
                one_step(low, active)
            else:

                def body(step, carry, active=active):
                    one_step(step, active)
                    return carry

                lax.fori_loop(low, high, body, 0)

    def kernel_tile(source):
        step = min(128, panels)

        def some_rows(index, carry):
            rows = pl.ds(pl.multiple_of(index * step, step), step)
            values = columns[rows, :]
            distance = jnp.zeros((step, panels), jnp.float32)
            for component in range(3):
                gap = geo[component : component + 1, :] - values[:, component : component + 1]
                distance = distance + gap * gap
            soft = distance + 0.5 * (geo[3:4, :] + values[:, 3:4])
            tile[rows, :] = (inv_four_pi * lax.rsqrt(soft)).astype(jnp.bfloat16)
            return carry

        columns[...] = jnp.transpose(source)
        lax.fori_loop(0, panels // step, some_rows, 0)

    def project_part(half, source, sizes, barrier=None):
        def some(rows):
            part[half, rows, :] = jnp.dot(
                source[rows, :], sorted_basis[...], preferred_element_type=jnp.float32
            )

        if share % 16 == 0:
            for peer in peers:
                some(pl.ds(pl.multiple_of(peer * share, 16), share))
        else:
            some(pl.ds(0, count))
        if barrier is not None:
            pl.semaphore_wait(barrier, blocks - 1 + levels)
        for piece in sizes:
            for copy in part_copies(half, *piece):
                copy.start()
        if share % 16 == 0:
            some(pl.ds(pl.multiple_of(my_blk * share, 16), share))

    def pieces(chunks):
        found, start = [], 0
        for size in [rows * chunk for rows in chunks] + [share]:
            size = min(size, share - start)
            if size > 0:
                found.append((start, size, len(found)))
                start += size
        return found

    probe_sizes, sketch_sizes = pieces([1, 2, 3]), pieces([2])

    order_load.wait()
    places = lax.broadcasted_iota(jnp.int32, (panels, panels), 0)
    chosen = jnp.where(places == order[...], 1.0, 0.0).astype(jnp.bfloat16)
    basis_load.wait()
    mats_load.start()
    sorted_basis[...] = jnp.dot(
        chosen, basis[...], preferred_element_type=jnp.float32
    ).astype(jnp.bfloat16)
    probe_load.wait()
    project_part(0, probe, probe_sizes, barrier)
    for load in geo_loads:
        load.wait()
    scaled[...] = (
        (geo[3:4, :] * probe[...].astype(jnp.float32)).astype(jnp.bfloat16).astype(jnp.float32)
    )
    for copy in geo_copies + scaled_copies:
        copy.start()
    mats_load.wait()
    full_load.start()

    for piece in probe_sizes:
        first_level(0, *piece)
    def own_near():
        near[...] = jnp.dot(
            scaled[...].astype(jnp.bfloat16), tile[...], preferred_element_type=jnp.float32
        )

    def peer_tile(index):
        geo_copies[index].wait_recv()
        kernel_tile(geo_in[index])

    def peer_near(index):
        scaled_copies[index].wait_recv()
        near[...] += jnp.dot(
            scaled_in[index].astype(jnp.bfloat16), tile[...], preferred_element_type=jnp.float32
        )
        if index == blocks - 2:
            full_load.wait()
            off[...] = (full[...].astype(jnp.float32) - near[...]).astype(jnp.bfloat16)

    def own_block():
        kernel_tile(geo[...])
        own_near()

    def peer_block(index):
        peer_tile(index)
        peer_near(index)

    tasks = [own_block]
    tasks += [functools.partial(peer_block, index) for index in range(blocks - 1)]
    tasks.append(lambda: project_part(1, off, sketch_sizes))
    tasks += [functools.partial(first_level, 1, *piece) for piece in sketch_sizes]
    early = min(len(tasks) - 1, per_half)
    for step, task in enumerate(tasks):
        task()
        if step < early:
            steps(step, step + 1)
    steps(early, total + lag * (levels - 1))
    for level in range(levels):
        pltpu.make_async_remote_copy(
            src_ref=going.at[level], dst_ref=coming.at[level],
            send_sem=level_send.at[level], recv_sem=level_recv.at[level, 0],
            device_id={"leaf": partners[level]}, device_id_type=MESH,
        ).wait_send()
    for half in range(2):
        for copy in result_copies(half, pl.ds(0, share)):
            copy.wait()
        for copy in part_copies(half, 0, share):
            copy.wait_send()
    for copy in geo_copies + scaled_copies:
        copy.wait_send()


def write_out(pieces, off, nested, off_hbm, nested_hbm, sem):
    rows = nested.shape[2] // pieces
    copies = [
        pltpu.make_async_copy(
            nested.at[0, half, pl.ds(piece * rows, rows)],
            nested_hbm.at[0, half, pl.ds(piece * rows, rows)],
            sem.at[half * pieces + piece],
        )
        for half in range(2)
        for piece in range(pieces)
    ]
    copies.append(pltpu.make_async_copy(off, off_hbm, sem.at[2 * pieces]))
    for copy in copies:
        copy.start()
    for copy in copies:
        copy.wait()


def shards(positions, panel_areas, probe_cols, full_sketch, tree_order, leaf_basis, transfer_mats):
    panels = positions.shape[3]
    count = probe_cols.shape[0]
    width = leaf_basis.shape[3]
    levels = transfer_mats.shape[1]
    blocks = lax.axis_size("blk")
    share = count // blocks
    chunk = chunk_rows(share)
    total = 2 * share // chunk
    f32, b16 = jnp.float32, jnp.bfloat16
    dma = pltpu.SemaphoreType.DMA
    whole = pl.BlockSpec(memory_space=pltpu.VMEM)
    hbm = pl.BlockSpec(memory_space=pltpu.HBM)
    offdiag, nested = pl.pallas_call(
        functools.partial(kernel, blocks, levels, chunk),
        out_shape=(
            pltpu.VMEM((count, panels), b16),
            pltpu.VMEM((1, 2, count, width), f32),
        ),
        in_specs=[hbm] * 7,
        out_specs=(whole, whole),
        scratch_shapes=[
            pltpu.VMEM((1, panels), jnp.int32),
            pltpu.VMEM((count, panels), b16),
            pltpu.VMEM((count, panels), b16),
            pltpu.VMEM((panels, width), b16),
            pltpu.VMEM((levels, width, width), b16),
            pltpu.VMEM((panels, width), b16),
            pltpu.VMEM((panels, panels), b16),
            pltpu.VMEM((8, panels), f32),
            pltpu.VMEM((blocks - 1, 8, panels), f32),
            pltpu.VMEM((panels, 8), f32),
            pltpu.VMEM((count, panels), f32),
            pltpu.VMEM((blocks - 1, count, panels), f32),
            pltpu.VMEM((count, panels), f32),
            pltpu.VMEM((2, count, width), f32),
            pltpu.VMEM((2, blocks - 1, share, width), f32),
            pltpu.VMEM((levels, 2 * share, width), f32),
            pltpu.VMEM((levels, 2 * share, width), f32),
            dma((9,)),
            dma((blocks - 1,)), dma((blocks - 1,)),
            dma((blocks - 1,)), dma((blocks - 1,)),
            dma((2, blocks - 1)), dma((2, blocks - 1, 4)),
            dma((levels,)), dma((levels, total)),
            dma((2, blocks - 1)), dma((2, blocks - 1)),
        ],
        compiler_params=pltpu.CompilerParams(
            collective_id=0, has_side_effects=True, vmem_limit_bytes=58 * 2**20
        ),
    )(
        positions,
        panel_areas,
        tree_order,
        probe_cols.reshape(count, panels),
        full_sketch.reshape(count, panels),
        leaf_basis.reshape(panels, width),
        transfer_mats.reshape(levels, width, width),
    )
    pieces = 4
    offdiag, nested = pl.pallas_call(
        functools.partial(write_out, pieces),
        out_shape=(
            jax.ShapeDtypeStruct((count, panels), b16),
            jax.ShapeDtypeStruct((1, 2, count, width), f32),
        ),
        in_specs=(whole, whole),
        out_specs=(hbm, hbm),
        scratch_shapes=[dma((1 + 2 * pieces,))],
        compiler_params=pltpu.CompilerParams(vmem_limit_bytes=2**20),
    )(offdiag, nested)
    return (offdiag.reshape(count, 1, 1, panels), nested)


def solution(mesh):
    in_specs = (
        P(None, "leaf", "blk", None),
        P("leaf", "blk", None),
        P(None, "leaf", "blk", None),
        P(None, "leaf", "blk", None),
        P("leaf", "blk", None),
        P("leaf", "blk", None, None),
        P("leaf", None, None, None),
    )
    out_specs = (P(None, "leaf", "blk", None), P("leaf", None, None, None))
    return jax.shard_map(shards, mesh=mesh, in_specs=in_specs, out_specs=out_specs, check_vma=False)
```

```python
import functools
import math

import jax
import jax.numpy as jnp
from jax import lax
from jax.experimental import pallas as pl
from jax.experimental.pallas import tpu as pltpu
from jax.sharding import PartitionSpec as P

MESH = pl.DeviceIdType.MESH
inv_four_pi = 1.0 / (4.0 * math.pi)


def chunk_rows(share):
    return max(rows for rows in range(8, min(share, 24) + 1, 8) if share % rows == 0)


def leaf_partner(me, level):
    step = 2**level
    return me + step * (1 - 2 * lax.rem(lax.div(me, step), 2))


def kernel(
    blocks, levels, chunk,
    pos_hbm, area_hbm, order_hbm, probe_hbm, full_hbm, basis_hbm, mats_hbm,
    off, nested,
    order, probe, full, basis, mats, sorted_basis, tile, geo, geo_in, columns, scaled, scaled_in,
    near, part, part_in, going, coming,
    load_sem, geo_send, geo_recv, scaled_send, scaled_recv, part_send, part_recv,
    level_send, level_recv, done_send, done_recv,
):
    count, panels = probe.shape
    share = count // blocks
    per_half = share // chunk
    lag = 4
    total = 2 * per_half
    my_blk = lax.axis_index("blk")
    my_leaf = lax.axis_index("leaf")
    peers = [lax.rem(my_blk + distance, blocks) for distance in range(1, blocks)]
    partners = [leaf_partner(my_leaf, level) for level in range(levels)]

    loads = [
        pltpu.make_async_copy(source, target, load_sem.at[index])
        for index, (source, target) in enumerate(
            [
                (order_hbm.at[0], order), (basis_hbm, basis), (probe_hbm, probe),
                (area_hbm.at[0], geo.at[pl.ds(3, 1)]),
            ]
            + [(pos_hbm.at[axis, 0], geo.at[pl.ds(axis, 1)]) for axis in range(3)]
            + [(mats_hbm, mats), (full_hbm, full)]
        )
    ]
    order_load, basis_load, probe_load, *geo_loads, mats_load, full_load = loads
    barrier = pltpu.get_barrier_semaphore()
    for peer in peers:
        pl.semaphore_signal(barrier, inc=1, device_id={"blk": peer}, device_id_type=MESH)
    for partner in partners:
        pl.semaphore_signal(barrier, inc=1, device_id={"leaf": partner}, device_id_type=MESH)
    geo[...] = jnp.zeros_like(geo)
    for load in [order_load, basis_load, probe_load] + geo_loads:
        load.start()

    def to_peers(source, target, send, recv):
        return [
            pltpu.make_async_remote_copy(
                src_ref=source, dst_ref=target.at[index], send_sem=send.at[index],
                recv_sem=recv.at[index], device_id={"blk": peer}, device_id_type=MESH,
            )
            for index, peer in enumerate(peers)
        ]

    def part_copies(half, start, size, place=0):
        return [
            pltpu.make_async_remote_copy(
                src_ref=part.at[half, pl.ds(pl.multiple_of(peer * share + start, 8), size)],
                dst_ref=part_in.at[half, index, pl.ds(start, size)],
                send_sem=part_send.at[half, index],
                recv_sem=part_recv.at[half, index, place],
                device_id={"blk": peer}, device_id_type=MESH,
            )
            for index, peer in enumerate(peers)
        ]

    geo_copies = to_peers(geo, geo_in, geo_send, geo_recv)
    scaled_copies = to_peers(scaled, scaled_in, scaled_send, scaled_recv)

    def chunk_slice(position):
        return pl.ds(pl.multiple_of(position * chunk, 8), chunk)

    def exchange(level, position):
        rows = chunk_slice(position)
        return pltpu.make_async_remote_copy(
            src_ref=going.at[level, rows], dst_ref=coming.at[level, rows],
            send_sem=level_send.at[level], recv_sem=level_recv.at[level, position],
            device_id={"leaf": partners[level]}, device_id_type=MESH,
        )

    def result_copies(half, rows):
        return [
            pltpu.make_async_remote_copy(
                src_ref=nested.at[0, 1 - half, rows], dst_ref=nested.at[0, 1 - half, rows],
                send_sem=done_send.at[half, index], recv_sem=done_recv.at[half, index],
                device_id={"blk": peer}, device_id_type=MESH,
            )
            for index, peer in enumerate(peers)
        ]

    def project(value, level):
        rows = value.shape[0]
        high = value.astype(jnp.bfloat16).astype(jnp.float32)
        both = jnp.concatenate([high, value - high], axis=0).astype(jnp.bfloat16)
        product = jnp.dot(both, mats[level], preferred_element_type=jnp.float32)
        return product[:rows] + product[rows:]

    def first_level(half, start, size, place):
        for copy in part_copies(half, start, size, place):
            copy.wait_recv()
        mine = pl.multiple_of(my_blk * share + start, 8)
        value = part[half, pl.ds(mine, size), :]
        for index in range(blocks - 1):
            value = value + part_in[half, index, pl.ds(start, size), :]
        going[0, pl.ds(half * share + start, size), :] = project(value, 0)

        def send(position, carry):
            exchange(0, position).start()
            return carry

        first = (half * share + start) // chunk
        lax.fori_loop(first, first + size // chunk, send, 0)

    def one_step(step, active):
        for level, on in enumerate(active):
            if on:
                exchange(level, step - lag * level).wait_recv()
        values = [
            going[level, chunk_slice(step - lag * level), :]
            + coming[level, chunk_slice(step - lag * level), :]
            for level in range(levels)
            if active[level]
        ]
        results = [
            project(value, level + 1) if level < levels - 1 else value
            for value, level in zip(values, [level for level in range(levels) if active[level]])
        ]
        for result, level in zip(results, [level for level in range(levels) if active[level]]):
            position = step - lag * level
            if level < levels - 1:
                going[level + 1, chunk_slice(position), :] = result
                exchange(level + 1, position).start()
            else:
                half = lax.div(position, per_half)
                start = my_blk * share + lax.rem(position, per_half) * chunk
                rows = pl.ds(pl.multiple_of(start, 8), chunk)
                nested[0, 1 - half, rows, :] = result
                for copy in result_copies(half, rows):
                    copy.start()

    def steps(start, stop):
        edges = sorted({lag * level for level in range(levels)})
        edges = sorted(set(edges + [edge + total for edge in edges] + [start, stop]))
        for low, high in zip(edges, edges[1:]):
            if low < start or high > stop:
                continue
            active = [lag * level <= low < total + lag * level for level in range(levels)]
            if high - low <= 1:
                one_step(low, active)
            else:

                def body(step, carry, active=active):
                    one_step(step, active)
                    return carry

                lax.fori_loop(low, high, body, 0)

    def kernel_tile(source):
        step = min(128, panels)

        def some_rows(index, carry):
            rows = pl.ds(pl.multiple_of(index * step, step), step)
            values = columns[rows, :]
            distance = jnp.zeros((step, panels), jnp.float32)
            for component in range(3):
                gap = geo[component : component + 1, :] - values[:, component : component + 1]
                distance = distance + gap * gap
            soft = distance + 0.5 * (geo[3:4, :] + values[:, 3:4])
            tile[rows, :] = (inv_four_pi * lax.rsqrt(soft)).astype(jnp.bfloat16)
            return carry

        columns[...] = jnp.transpose(source)
        lax.fori_loop(0, panels // step, some_rows, 0)

    def project_part(half, source, sizes, barrier=None):
        def some(rows):
            part[half, rows, :] = jnp.dot(
                source[rows, :], sorted_basis[...], preferred_element_type=jnp.float32
            )

        if share % 16 == 0:
            for peer in peers:
                some(pl.ds(pl.multiple_of(peer * share, 16), share))
        else:
            some(pl.ds(0, count))
        if barrier is not None:
            pl.semaphore_wait(barrier, blocks - 1 + levels)
        for piece in sizes:
            for copy in part_copies(half, *piece):
                copy.start()
        if share % 16 == 0:
            some(pl.ds(pl.multiple_of(my_blk * share, 16), share))

    def pieces(chunks):
        found, start = [], 0
        for size in [rows * chunk for rows in chunks] + [share]:
            size = min(size, share - start)
            if size > 0:
                found.append((start, size, len(found)))
                start += size
        return found

    probe_sizes, sketch_sizes = pieces([1, 3, 4]), pieces([4])

    order_load.wait()
    places = lax.broadcasted_iota(jnp.int32, (panels, panels), 0)
    chosen = jnp.where(places == order[...], 1.0, 0.0).astype(jnp.bfloat16)
    basis_load.wait()
    mats_load.start()
    sorted_basis[...] = jnp.dot(
        chosen, basis[...], preferred_element_type=jnp.float32
    ).astype(jnp.bfloat16)
    probe_load.wait()
    project_part(0, probe, probe_sizes, barrier)
    for load in geo_loads:
        load.wait()
    scaled[...] = (
        (geo[3:4, :] * probe[...].astype(jnp.float32)).astype(jnp.bfloat16).astype(jnp.float32)
    )
    for copy in geo_copies + scaled_copies:
        copy.start()
    mats_load.wait()
    full_load.start()

    for piece in probe_sizes:
        first_level(0, *piece)
    def own_near():
        near[...] = jnp.dot(
            scaled[...].astype(jnp.bfloat16), tile[...], preferred_element_type=jnp.float32
        )

    def peer_tile(index):
        geo_copies[index].wait_recv()
        kernel_tile(geo_in[index])

    def peer_near(index):
        scaled_copies[index].wait_recv()
        near[...] += jnp.dot(
            scaled_in[index].astype(jnp.bfloat16), tile[...], preferred_element_type=jnp.float32
        )
        if index == blocks - 2:
            full_load.wait()
            off[...] = (full[...].astype(jnp.float32) - near[...]).astype(jnp.bfloat16)

    tasks = [lambda: kernel_tile(geo[...]), own_near]
    for index in range(blocks - 1):
        tasks += [functools.partial(peer_tile, index), functools.partial(peer_near, index)]
    tasks.append(lambda: project_part(1, off, sketch_sizes))
    tasks += [functools.partial(first_level, 1, *piece) for piece in sketch_sizes]
    early = min(len(tasks) - 1, per_half)
    for step, task in enumerate(tasks):
        task()
        if step < early:
            steps(step, step + 1)
    steps(early, total + lag * (levels - 1))
    for level in range(levels):
        pltpu.make_async_remote_copy(
            src_ref=going.at[level], dst_ref=coming.at[level],
            send_sem=level_send.at[level], recv_sem=level_recv.at[level, 0],
            device_id={"leaf": partners[level]}, device_id_type=MESH,
        ).wait_send()
    for half in range(2):
        for copy in result_copies(half, pl.ds(0, share)):
            copy.wait()
        for copy in part_copies(half, 0, share):
            copy.wait_send()
    for copy in geo_copies + scaled_copies:
        copy.wait_send()


def write_out(pieces, off, nested, off_hbm, nested_hbm, sem):
    rows = nested.shape[2] // pieces
    copies = [
        pltpu.make_async_copy(
            nested.at[0, half, pl.ds(piece * rows, rows)],
            nested_hbm.at[0, half, pl.ds(piece * rows, rows)],
            sem.at[half * pieces + piece],
        )
        for half in range(2)
        for piece in range(pieces)
    ]
    copies.append(pltpu.make_async_copy(off, off_hbm, sem.at[2 * pieces]))
    for copy in copies:
        copy.start()
    for copy in copies:
        copy.wait()


def shards(positions, panel_areas, probe_cols, full_sketch, tree_order, leaf_basis, transfer_mats):
    panels = positions.shape[3]
    count = probe_cols.shape[0]
    width = leaf_basis.shape[3]
    levels = transfer_mats.shape[1]
    blocks = lax.axis_size("blk")
    share = count // blocks
    chunk = chunk_rows(share)
    total = 2 * share // chunk
    f32, b16 = jnp.float32, jnp.bfloat16
    dma = pltpu.SemaphoreType.DMA
    whole = pl.BlockSpec(memory_space=pltpu.VMEM)
    hbm = pl.BlockSpec(memory_space=pltpu.HBM)
    offdiag, nested = pl.pallas_call(
        functools.partial(kernel, blocks, levels, chunk),
        out_shape=(
            pltpu.VMEM((count, panels), b16),
            pltpu.VMEM((1, 2, count, width), f32),
        ),
        in_specs=[hbm] * 7,
        out_specs=(whole, whole),
        scratch_shapes=[
            pltpu.VMEM((1, panels), jnp.int32),
            pltpu.VMEM((count, panels), b16),
            pltpu.VMEM((count, panels), b16),
            pltpu.VMEM((panels, width), b16),
            pltpu.VMEM((levels, width, width), b16),
            pltpu.VMEM((panels, width), b16),
            pltpu.VMEM((panels, panels), b16),
            pltpu.VMEM((8, panels), f32),
            pltpu.VMEM((blocks - 1, 8, panels), f32),
            pltpu.VMEM((panels, 8), f32),
            pltpu.VMEM((count, panels), f32),
            pltpu.VMEM((blocks - 1, count, panels), f32),
            pltpu.VMEM((count, panels), f32),
            pltpu.VMEM((2, count, width), f32),
            pltpu.VMEM((2, blocks - 1, share, width), f32),
            pltpu.VMEM((levels, 2 * share, width), f32),
            pltpu.VMEM((levels, 2 * share, width), f32),
            dma((9,)),
            dma((blocks - 1,)), dma((blocks - 1,)),
            dma((blocks - 1,)), dma((blocks - 1,)),
            dma((2, blocks - 1)), dma((2, blocks - 1, 4)),
            dma((levels,)), dma((levels, total)),
            dma((2, blocks - 1)), dma((2, blocks - 1)),
        ],
        compiler_params=pltpu.CompilerParams(
            collective_id=0, has_side_effects=True, vmem_limit_bytes=58 * 2**20
        ),
    )(
        positions,
        panel_areas,
        tree_order,
        probe_cols.reshape(count, panels),
        full_sketch.reshape(count, panels),
        leaf_basis.reshape(panels, width),
        transfer_mats.reshape(levels, width, width),
    )
    pieces = 4
    offdiag, nested = pl.pallas_call(
        functools.partial(write_out, pieces),
        out_shape=(
            jax.ShapeDtypeStruct((count, panels), b16),
            jax.ShapeDtypeStruct((1, 2, count, width), f32),
        ),
        in_specs=(whole, whole),
        out_specs=(hbm, hbm),
        scratch_shapes=[dma((1 + 2 * pieces,))],
        compiler_params=pltpu.CompilerParams(vmem_limit_bytes=2**20),
    )(offdiag, nested)
    return (offdiag.reshape(count, 1, 1, panels), nested)


def solution(mesh):
    in_specs = (
        P(None, "leaf", "blk", None),
        P("leaf", "blk", None),
        P(None, "leaf", "blk", None),
        P(None, "leaf", "blk", None),
        P("leaf", "blk", None),
        P("leaf", "blk", None, None),
        P("leaf", None, None, None),
    )
    out_specs = (P(None, "leaf", "blk", None), P("leaf", None, None, None))
    return jax.shard_map(shards, mesh=mesh, in_specs=in_specs, out_specs=out_specs, check_vma=False)
```
